512 devices in a mesh: mesh: 128 (over z, x, y_hi), field: 4 (over y_lo, core).
Axes of the slice: x: 4, y: 8 (y_hi: 4, y_lo: 2; y = y_hi * 2 + y_lo), z: 8, core: 2. Of those that a mesh axis runs over, the one named last changes fastest.
Arguments:
- velocity: float32 [3, 512, 1024], P(None, ('mesh', 'field')), may hold values from -4 to 4
- pressure: float32 [512, 1024], P(('mesh', 'field')), may hold values from -128 to 128
- fields: bfloat16 [3, 256, 512, 1024], P(None, 'field', 'mesh'), may hold values from -1.8 to 1.8
- brownian: bfloat16 [3, 256, 512, 1024], P(None, 'field', 'mesh'), may hold values from -4 to 4
Outputs:
- new_fields: bfloat16 [3, 256, 512, 1024], P(None, 'field', 'mesh')
- new_velocity: float32 [3, 512, 1024], P(None, ('mesh', 'field'))
The draws below stay inside these ranges and needn't reach their ends.
All inputs are finite; a program needn't handle non-finite values.
Results may differ from the reference program's by a relative error of at most 0.001.
Values sent between devices are 32-bit elements; how exact they have to be, the bound alone decides.
No kernel may reach another device: no remote copies, remote signals or barrier semaphores. Data moves between devices by JAX's collectives and lax.ppermute only.
A program may use at most 64 MiB of HBM per device.

```python
import math
import jax
import jax.numpy as jnp
from jax import lax

NF = 256
NY = 32
NZ = 32
CXF = 1
SWEEPS = 4
PLANE = 1024
NX = 512


def draw_fields(key, part):
    scale_key, value_key = jax.random.split(jax.random.fold_in(key, 7), 2)
    log_scale = jax.random.uniform(scale_key, (3, 1, NX, PLANE), jnp.float32, math.log(0.3), math.log(1.75))
    node_scale = jnp.exp(log_scale)
    values = jax.random.uniform(value_key, (3, NF, NX, PLANE), jnp.float32, -1.0, 1.0)
    return (node_scale * values).astype(jnp.bfloat16)


def block_scale(rng, shape, cuts, low, high):
    def one(dim, shards_of):
        heights = jax.random.uniform(jax.random.fold_in(jax.random.fold_in(rng, 6), dim), (shards_of,), jnp.float32, low / len(cuts), high / len(cuts))
        return jnp.repeat(jnp.exp(heights), shape[dim] // shards_of).reshape((-1,) + (1,) * (len(shape) - dim - 1))

    gain = one(*cuts[0])
    for cut in cuts[1:]:
        gain = gain * one(*cut)
    return gain


def bell_draw(stream_key, shape, width, limit, cuts=(), kind=jnp.bfloat16):
    level = block_scale(stream_key, shape, cuts, -0.22, 0.18) if cuts else 1.0
    values = jax.random.normal(stream_key, shape, jnp.float32) * width * level
    return jnp.minimum(jnp.maximum(values, -limit), limit).astype(kind)


def setup_inputs(seed: int = 0) -> dict:
    arg_keys = jax.random.split(jax.random.key(seed), 5)
    velocity = bell_draw(arg_keys[0], (3, NX, PLANE), 1.0, 4.0, ((1, 512),), jnp.float32)
    pressure = bell_draw(arg_keys[1], (NX, PLANE), 32.0, 128.0, ((0, 512),), jnp.float32)
    fields = draw_fields(jax.random.fold_in(arg_keys[4], 71), 0)
    brownian = bell_draw(arg_keys[3], (3, NF, NX, PLANE), 1.0, 4.0, ((1, 4), (2, 128)))
    return {"velocity": velocity, "pressure": pressure, "fields": fields, "brownian": brownian}


time_step = 0.02
axial_weight = 400.0
transverse_weight = 40.0
weissenberg = 0.5
max_stretch = 50.0
polymer_viscosity = 40.0
noise_scale = (0.02 / 0.5) ** 0.5
diagonal_weight = 1.0 / 0.02 + 2.0 * 400.0 + 4.0 * 40.0
index_table = ((0, 1, 2), (1, 3, 4), (2, 4, 5))
component_pairs = ((0, 0), (0, 1), (0, 2), (1, 1), (1, 2), (2, 2))


def plane_shifts(values):
    extent = values.shape[-1]
    leading = [(0, 0)] * (values.ndim - 1)
    along_y = jnp.pad(values, leading + [(NZ, NZ)])
    along_z = jnp.pad(values, leading + [(1, 1)])
    column = lax.broadcasted_iota(jnp.int32, (extent,), 0) % NZ
    upper_keep = (column < NZ - 1).astype(values.dtype)
    lower_keep = (column > 0).astype(values.dtype)
    return along_y[..., 2 * NZ:], along_y[..., :extent], along_z[..., 2:] * upper_keep, along_z[..., :extent] * lower_keep


def derivatives(padded):
    interior = padded[:, 1:-1]
    y_plus, y_minus, z_plus, z_minus = plane_shifts(interior)
    return ((padded[:, 2:] - padded[:, :-2]) * 0.5, (y_plus - y_minus) * 0.5, (z_plus - z_minus) * 0.5)


def velocity_gradient(padded):
    stacked = jnp.stack(derivatives(padded), axis=1)
    return stacked.reshape(9, stacked.shape[2], stacked.shape[3])


def advance(fields, brownian, gradient):
    current = fields.astype(jnp.float32)
    increments = brownian.astype(jnp.float32)
    length_sq = current[0] * current[0] + current[1] * current[1] + current[2] * current[2]
    spring = 1.0 / (1.0 - length_sq / max_stretch)
    drift_terms = []
    for out_axis in range(3):
        stretch = gradient[3 * out_axis][None] * current[0] + gradient[3 * out_axis + 1][None] * current[1] + gradient[3 * out_axis + 2][None] * current[2]
        drift_terms.append(stretch - spring * current[out_axis] / (2.0 * weissenberg))
    advanced = current + time_step * jnp.stack(drift_terms) + noise_scale * increments
    new_sq = advanced[0] * advanced[0] + advanced[1] * advanced[1] + advanced[2] * advanced[2]
    new_spring = 1.0 / (1.0 - new_sq / max_stretch)
    partial_value = jnp.stack([jnp.sum(new_spring * advanced[left_axis] * advanced[right_axis], axis=0) for left_axis, right_axis in component_pairs])
    return advanced.astype(jnp.bfloat16), partial_value


def to_stress(summed):
    identity = jnp.array([1.0, 0.0, 0.0, 1.0, 0.0, 1.0], dtype=summed.dtype)[:, None, None]
    return (polymer_viscosity / weissenberg) * (summed / NF - identity)


def momentum_source(velocity, padded_pressure, padded_stress):
    pressure_grad = jnp.concatenate(derivatives(padded_pressure), axis=0)
    slopes = derivatives(padded_stress)
    divergence = jnp.stack([slopes[0][index_table[out_axis][0]] + slopes[1][index_table[out_axis][1]] + slopes[2][index_table[out_axis][2]] for out_axis in range(3)])
    return velocity / time_step - pressure_grad + divergence


def fluid_mask(offset, planes, total_planes, extent):
    position = offset + lax.broadcasted_iota(jnp.int32, (planes, extent), 0)
    across = lax.broadcasted_iota(jnp.int32, (planes, extent), 1) // NZ
    blocked = (position >= total_planes // 2) & ((across < NY // 4) | (across >= NY - NY // 4))
    return jnp.where(blocked, 0.0, 1.0).astype(jnp.float32)


def relax_step(padded, source, fluid):
    interior = padded[:, 1:-1]
    y_plus, y_minus, z_plus, z_minus = plane_shifts(interior)
    along_flow = padded[:, 2:] + padded[:, :-2]
    across_flow = y_plus + y_minus + z_plus + z_minus
    return fluid * (source + axial_weight * along_flow + transverse_weight * across_flow) / diagonal_weight


def reference(velocity, pressure, fields, brownian):
    stacked = jnp.concatenate([velocity, pressure[None]], axis=0)
    padded = jnp.pad(stacked, ((0, 0), (1, 1), (0, 0)))
    gradient = velocity_gradient(padded[:3])

    def one_block(number):
        first_plane = (number * CXF).astype(jnp.int32)
        return advance(lax.dynamic_slice_in_dim(fields, first_plane, CXF, 2),
                       lax.dynamic_slice_in_dim(brownian, first_plane, CXF, 2),
                       lax.dynamic_slice_in_dim(gradient, first_plane, CXF, 1))

    advanced, partial_value = lax.map(one_block, jnp.arange(NX // CXF, dtype=jnp.int32))
    new_fields = jnp.moveaxis(advanced, 0, 2).reshape(3, NF, NX, PLANE)
    summed = jnp.moveaxis(partial_value, 0, 1).reshape(6, NX, PLANE)
    stress = to_stress(summed)
    padded_stress = jnp.pad(stress, ((0, 0), (1, 1), (0, 0)))
    source = momentum_source(velocity, padded[3:], padded_stress)
    fluid = fluid_mask(0, NX, NX, PLANE)
    current = velocity
    for repeat in range(SWEEPS):
        current = relax_step(jnp.pad(current, ((0, 0), (1, 1), (0, 0))), source, fluid)
    return new_fields, current
```

```python
import functools

import jax
import jax.numpy as jnp
from jax import lax
from jax.experimental import pallas as pl
from jax.experimental.pallas import tpu as pltpu
from jax.sharding import PartitionSpec as P

f32 = jnp.float32
bf16 = jnp.bfloat16

NF = 256
TIME_STEP = 0.02
AXIAL = 400.0
TRANSVERSE = 40.0
MAX_STRETCH = 50.0
VISCOSITY = 40.0
WEISSENBERG = 0.5
NOISE = (0.02 / 0.5) ** 0.5
DIAGONAL = 1.0 / 0.02 + 2.0 * 400.0 + 4.0 * 40.0
SWEEPS = 4
INDEX = ((0, 1, 2), (1, 3, 4), (2, 4, 5))
DIAGONAL_PAIRS = (0, 3, 5)

PLANES = 4
CHUNKS = 4
UNROLL = 4
AXES = ("mesh", "field")


def lane_masks():
    lane = lax.broadcasted_iota(jnp.int32, (8, 128), 1)
    row = lax.broadcasted_iota(jnp.int32, (8, 128), 0)
    return dict(
        z_hi=(lane % 32) < 31,
        z_lo=(lane % 32) > 0,
        lane_hi=lane < 96,
        lane_lo=lane >= 32,
        row_hi=row < 7,
        row_lo=row > 0,
        channel=(row >= 2) & (row < 6),
    )


def shift_z(v, masks):
    plus = jnp.where(masks["z_hi"], pltpu.roll(v, 127, 1), 0.0)
    minus = jnp.where(masks["z_lo"], pltpu.roll(v, 1, 1), 0.0)
    return plus, minus


def shift_y(v, masks):
    ahead = pltpu.roll(v, 96, 1)
    behind = pltpu.roll(v, 32, 1)
    next_row = jnp.where(masks["row_hi"], pltpu.roll(ahead, 7, 0), 0.0)
    last_row = jnp.where(masks["row_lo"], pltpu.roll(behind, 1, 0), 0.0)
    return jnp.where(masks["lane_hi"], ahead, next_row), jnp.where(masks["lane_lo"], behind, last_row)


def slope_y(v, masks):
    plus, minus = shift_y(v, masks)
    return (plus - minus) * 0.5


def slope_z(v, masks):
    plus, minus = shift_z(v, masks)
    return (plus - minus) * 0.5


def around(v, masks):
    y_plus, y_minus = shift_y(v, masks)
    z_plus, z_minus = shift_z(v, masks)
    return (y_plus + y_minus) + (z_plus + z_minus)


def advance(f, b, g):
    length_sq = f[0] * f[0] + f[1] * f[1] + f[2] * f[2]
    kept = 1.0 - (TIME_STEP * MAX_STRETCH / (2.0 * WEISSENBERG)) * pl.reciprocal(MAX_STRETCH - length_sq, approx=False)
    a = []
    for o in range(3):
        row = [g[3 * o + c] for c in range(3)]
        row[o] = row[o] + kept
        a.append(row[0] * f[0] + row[1] * f[1] + row[2] * f[2] + NOISE * b[o])
    s = [x * x for x in a]
    r = pl.reciprocal(MAX_STRETCH - (s[0] + s[1] + s[2]), approx=False)
    p0 = r * a[0]
    p1 = r * a[1]
    return a, (r * s[0], p0 * a[1], p0 * a[2], r * s[1], p1 * a[2], r * s[2])


def step_kernel(slabs, around_ref, velocity_ref, pressure_ref, f_hbm, b_hbm, nf_hbm, out_ref,
                f_buf, b_buf, n_buf, grad, sums, in_sem, out_sem):
    pairs = f_buf.shape[1]
    per = pairs // CHUNKS

    def loads(ch):
        some = pl.ds(ch * per, per)
        return [
            pltpu.make_async_copy(src.at[c, some, h], buf.at[c, some, pl.ds(4 * h, 4), :], in_sem.at[ch, 6 * w + 2 * c + h])
            for w, (src, buf) in enumerate(((f_hbm, f_buf), (b_hbm, b_buf)))
            for c in range(3)
            for h in range(2)
        ]

    def stores(ch):
        some = pl.ds(ch * per, per)
        return [
            pltpu.make_async_copy(n_buf.at[c, some, pl.ds(4 * h, 4), :], nf_hbm.at[c, some, h], out_sem.at[ch, 2 * c + h])
            for c in range(3)
            for h in range(2)
        ]

    for ch in range(CHUNKS):
        for copy in loads(ch):
            copy.start()

    slab = lax.axis_index("mesh")
    mine = lax.axis_index("field")
    masks = lane_masks()

    for q in range(PLANES):
        for a in range(3):
            centre = around_ref[q + 1, a]
            slopes = (
                (around_ref[q + 2, a] - around_ref[q, a]) * 0.5,
                slope_y(centre, masks),
                slope_z(centre, masks),
            )
            for c in range(3):
                value = slopes[c] * TIME_STEP
                grad[3 * a + c, pl.ds(q, 8, stride=8), :] = value
                grad[3 * a + c, pl.ds(q + 4, 8, stride=8), :] = value

    for ch in range(CHUNKS):
        for copy in loads(ch):
            copy.wait()

        def block(j, carry):
            rows = pl.ds(pl.multiple_of(8 * j, 8), 8)
            lanes = pl.ds(pl.multiple_of(128 * j, 128), 128)
            g = [grad[k, rows, :] for k in range(9)]

            def some_fields(i, acc):
                for u in range(UNROLL):
                    n = ch * per + i * UNROLL + u
                    f = [f_buf[c, n, :, lanes].astype(f32) for c in range(3)]
                    b = [b_buf[c, n, :, lanes].astype(f32) for c in range(3)]
                    a, products = advance(f, b, g)
                    for c in range(3):
                        n_buf[c, n, :, lanes] = a[c].astype(bf16)
                    acc = tuple(x + y for x, y in zip(acc, products))
                return acc

            if ch:
                acc = tuple(sums[k, rows, :] for k in range(6))
            else:
                acc = tuple(jnp.zeros((8, 128), f32) for _ in range(6))
            acc = lax.fori_loop(0, per // UNROLL, some_fields, acc)
            for k in range(6):
                sums[k, rows, :] = acc[k]
            return carry

        lax.fori_loop(0, 8, block, 0)
        for copy in stores(ch):
            copy.start()

    scale = VISCOSITY / WEISSENBERG / NF * MAX_STRETCH
    stress = []
    for k in range(6):
        rows = []
        for q in range(PLANES):
            total = sums[k, pl.ds(q, 8, stride=8), :] + sums[k, pl.ds(q + 4, 8, stride=8), :]
            total = total * scale
            if k in DIAGONAL_PAIRS:
                total = total - VISCOSITY / WEISSENBERG / 4
            rows.append(total)
        stress.append(rows)

    own = [mine == q for q in range(PLANES)]
    zero = jnp.zeros((8, 128), f32)
    pressure = [jnp.where(own[q], pressure_ref[...], 0.0) for q in range(PLANES)]
    start = [[jnp.where(own[q], velocity_ref[a], 0.0) for q in range(PLANES)] for a in range(3)]

    def at(values, q):
        return values[q] if 0 <= q < PLANES else None

    def add(x, y):
        return y if x is None else x if y is None else x + y

    def halfway(values, q):
        plus, minus = at(values, q + 1), at(values, q - 1)
        if plus is None:
            return None if minus is None else minus * -0.5
        return plus * 0.5 if minus is None else (plus - minus) * 0.5

    first = -(SWEEPS)
    count = PLANES + 2 * SWEEPS
    fluid = []
    for q in range(first, first + count):
        plane = slab * PLANES + q
        inside = (plane >= 0) & (plane < slabs * PLANES)
        wide = plane < slabs * PLANES // 2
        value = jnp.where(masks["channel"] | wide, 1.0 / DIAGONAL, 0.0)
        fluid.append(jnp.where(inside, value, 0.0))

    for a in range(3):
        source = {}
        for q in range(-1, PLANES + 1):
            total = halfway(stress[INDEX[a][0]], q)
            if a == 0:
                total = total - halfway(pressure, q) if total is not None else None
            if 0 <= q < PLANES:
                inner = slope_y(stress[INDEX[a][1]][q], masks) + slope_z(stress[INDEX[a][2]][q], masks)
                if a == 1:
                    inner = inner - slope_y(pressure[q], masks)
                if a == 2:
                    inner = inner - slope_z(pressure[q], masks)
                total = total + inner + start[a][q] * (1.0 / TIME_STEP)
            source[q] = total
        current = {q: start[a][q] for q in range(PLANES)}
        for sweep in range(SWEEPS):
            later = {}
            for q in range(-1 - sweep, PLANES + 1 + sweep):
                total = source.get(q)
                along = add(current.get(q - 1), current.get(q + 1))
                if along is not None:
                    total = add(total, AXIAL * along)
                if q in current:
                    total = add(total, TRANSVERSE * around(current[q], masks))
                later[q] = total * fluid[q - first]
            current = later
        for q in range(first, first + count):
            out_ref[q - first, a] = current[q]

    for ch in range(CHUNKS):
        for copy in stores(ch):
            copy.wait()


def step(planes6, velocity, pressure, fields, brownian):
    n = fields.shape[1] // 2
    split = (3, n, 2, PLANES, 1024)
    slabs = lax.axis_size("mesh")
    vmem = pl.BlockSpec(memory_space=pltpu.VMEM)
    hbm = pl.BlockSpec(memory_space=pl.ANY)
    new_fields, shares = pl.pallas_call(
        functools.partial(step_kernel, slabs),
        out_shape=(
            jax.ShapeDtypeStruct(split, bf16),
            jax.ShapeDtypeStruct((PLANES + 2 * SWEEPS, 3, 8, 128), f32),
        ),
        in_specs=[vmem, vmem, vmem, hbm, hbm],
        out_specs=[hbm, vmem],
        scratch_shapes=[
            pltpu.VMEM((3, n, 8, 1024), bf16),
            pltpu.VMEM((3, n, 8, 1024), bf16),
            pltpu.VMEM((3, n, 8, 1024), bf16),
            pltpu.VMEM((9, 64, 128), f32),
            pltpu.VMEM((6, 64, 128), f32),
            pltpu.SemaphoreType.DMA((CHUNKS, 12)),
            pltpu.SemaphoreType.DMA((CHUNKS, 6)),
        ],
        compiler_params=pltpu.CompilerParams(vmem_limit_bytes=24 << 20),
    )(planes6, velocity, pressure, fields.reshape(split), brownian.reshape(split))
    return new_fields.reshape(fields.shape), shares


def body(velocity, pressure, fields, brownian):
    slabs = lax.axis_size("mesh")
    total = slabs * 4
    slab = lax.axis_index("mesh")
    mine = lax.axis_index("field")
    low = mine < 2
    core = mine % 2
    cores = [[i, i + 1] for i in range(0, total, 2)]
    inner = [[i, i + 2] for s in range(0, total, 4) for i in (s, s + 1)]
    outer = [[i, (i + 2) % total] for s in range(2, total + 2, 4) for i in (s, s + 1)]

    def gather(x, groups):
        return lax.all_gather(x, AXES, axis=0, axis_index_groups=groups)

    def other(x, first):
        return jnp.where(first, x[1], x[0])

    own = velocity.reshape(3, 8, 128)
    near = gather(own, outer)
    near = gather(near, cores)
    left = jnp.where(slab > 0, near[1, 0], 0.0)
    right = jnp.where(slab < slabs - 1, near[0, 1], 0.0)
    send = jnp.where(
        low,
        jnp.stack([left, near[0, 1], near[1, 1]]),
        jnp.stack([near[0, 0], near[1, 0], right]),
    )
    planes6 = gather(send, inner).reshape(6, 3, 8, 128)

    new_fields, shares = step(planes6, own, pressure.reshape(8, 128), fields, brownian)

    both = gather(shares, cores).reshape(2, 3, 2, 2, 3, 8, 128)
    chip = both[0] + both[1]
    chip = jnp.where(core == 0, chip[:, :, 0], chip[:, :, 1])
    low_side = jnp.stack([chip[1, 0], chip[0, 0], chip[0, 1]])
    high_side = jnp.stack([chip[1, 1], chip[2, 0], chip[2, 1]])
    kept = jnp.where(low, low_side, high_side)
    kept = kept + other(gather(jnp.where(low, high_side, low_side), inner), low)
    arrived = other(gather(kept[1:], outer), ~low)
    mine_sum = kept[0] + jnp.where(low, arrived[0], arrived[1])
    passed = jnp.where(low, arrived[1], arrived[0])
    result = mine_sum + other(gather(passed, inner), low)
    return new_fields, result.reshape(velocity.shape)


def solution(mesh):
    placed = (
        P(None, ("mesh", "field"), None),
        P(("mesh", "field"), None),
        P(None, "field", "mesh", None),
        P(None, "field", "mesh", None),
    )
    return jax.shard_map(
        body,
        mesh=mesh,
        in_specs=placed,
        out_specs=(P(None, "field", "mesh", None), P(None, ("mesh", "field"), None)),
        check_vma=False,
    )
```

```python
import functools

import jax
import jax.numpy as jnp
from jax import lax
from jax.experimental import pallas as pl
from jax.experimental.pallas import tpu as pltpu
from jax.sharding import PartitionSpec as P

f32 = jnp.float32
bf16 = jnp.bfloat16

NF = 256
TIME_STEP = 0.02
AXIAL = 400.0
TRANSVERSE = 40.0
MAX_STRETCH = 50.0
VISCOSITY = 40.0
WEISSENBERG = 0.5
NOISE = (0.02 / 0.5) ** 0.5
DIAGONAL = 1.0 / 0.02 + 2.0 * 400.0 + 4.0 * 40.0
SWEEPS = 4
INDEX = ((0, 1, 2), (1, 3, 4), (2, 4, 5))
DIAGONAL_PAIRS = (0, 3, 5)

PLANES = 4
CHUNKS = 4
AXES = ("mesh", "field")


def lane_masks():
    lane = lax.broadcasted_iota(jnp.int32, (8, 128), 1)
    row = lax.broadcasted_iota(jnp.int32, (8, 128), 0)
    return dict(
        z_hi=(lane % 32) < 31,
        z_lo=(lane % 32) > 0,
        lane_hi=lane < 96,
        lane_lo=lane >= 32,
        row_hi=row < 7,
        row_lo=row > 0,
        channel=(row >= 2) & (row < 6),
    )


def shift_z(v, masks):
    plus = jnp.where(masks["z_hi"], pltpu.roll(v, 127, 1), 0.0)
    minus = jnp.where(masks["z_lo"], pltpu.roll(v, 1, 1), 0.0)
    return plus, minus


def shift_y(v, masks):
    ahead = pltpu.roll(v, 96, 1)
    behind = pltpu.roll(v, 32, 1)
    next_row = jnp.where(masks["row_hi"], pltpu.roll(ahead, 7, 0), 0.0)
    last_row = jnp.where(masks["row_lo"], pltpu.roll(behind, 1, 0), 0.0)
    return jnp.where(masks["lane_hi"], ahead, next_row), jnp.where(masks["lane_lo"], behind, last_row)


def slope_y(v, masks):
    plus, minus = shift_y(v, masks)
    return (plus - minus) * 0.5


def slope_z(v, masks):
    plus, minus = shift_z(v, masks)
    return (plus - minus) * 0.5


def around(v, masks):
    y_plus, y_minus = shift_y(v, masks)
    z_plus, z_minus = shift_z(v, masks)
    return (y_plus + y_minus) + (z_plus + z_minus)


def chunk(ch, pairs):
    per = pairs // CHUNKS
    return pl.ds(ch * per, per)


def loads(ch, sources, buffers, sem):
    some = chunk(ch, buffers[0].shape[1])
    return [
        pltpu.make_async_copy(src.at[c, some, h], buf.at[c, some, pl.ds(4 * h, 4), :], sem.at[ch, 6 * w + 2 * c + h])
        for w, (src, buf) in enumerate(zip(sources, buffers))
        for c in range(3)
        for h in range(2)
    ]


def stores(ch, buf, dst, sem):
    some = chunk(ch, buf.shape[1])
    return [
        pltpu.make_async_copy(buf.at[c, some, pl.ds(4 * h, 4), :], dst.at[c, some, h], sem.at[ch, 2 * c + h])
        for c in range(3)
        for h in range(2)
    ]


def relax_kernel(velocity_ref, pressure_ref, f_hbm, b_hbm, f_ref, base_ref, local_ref, b_buf, sem):
    pairs = b_buf.shape[1]
    per = pairs // CHUNKS
    for ch in range(CHUNKS):
        for copy in loads(ch, (f_hbm, b_hbm), (f_ref, b_buf), sem):
            copy.start()
    for a in range(3):
        local_ref[a] = velocity_ref[a]
    local_ref[3] = pressure_ref[...]
    for ch in range(CHUNKS):
        for copy in loads(ch, (f_hbm, b_hbm), (f_ref, b_buf), sem):
            copy.wait()

        def block(j, carry):
            lanes = pl.ds(pl.multiple_of(128 * j, 128), 128)
            for u in range(per):
                n = ch * per + u
                f = [f_ref[c, n, :, lanes].astype(f32) for c in range(3)]
                length_sq = f[0] * f[0] + f[1] * f[1] + f[2] * f[2]
                pull = TIME_STEP * MAX_STRETCH / (2.0 * WEISSENBERG) * pltpu.reciprocal(MAX_STRETCH - length_sq)
                kept = 1.0 - pull
                for c in range(3):
                    base_ref[c, n, :, lanes] = kept * f[c] + NOISE * b_buf[c, n, :, lanes].astype(f32)
            return carry

        lax.fori_loop(0, 8, block, 0)


def relax(velocity, pressure, fields, brownian):
    n = fields.shape[1] // 2
    split = (3, n, 2, PLANES, 1024)
    flat = (3, n, 8, 1024)
    vmem = pl.BlockSpec(memory_space=pltpu.VMEM)
    hbm = pl.BlockSpec(memory_space=pl.ANY)
    return pl.pallas_call(
        relax_kernel,
        out_shape=(
            jax.ShapeDtypeStruct(flat, bf16),
            jax.ShapeDtypeStruct(flat, f32),
            jax.ShapeDtypeStruct((4, 8, 128), f32),
        ),
        in_specs=[vmem, vmem, hbm, hbm],
        out_specs=[vmem, vmem, vmem],
        scratch_shapes=[pltpu.VMEM(flat, bf16), pltpu.SemaphoreType.DMA((CHUNKS, 12))],
        compiler_params=pltpu.CompilerParams(vmem_limit_bytes=24 << 20),
        cost_estimate=pl.CostEstimate(flops=10_000_000, bytes_accessed=8_000_000, transcendentals=0),
    )(velocity, pressure, fields.reshape(split), brownian.reshape(split))


def share_kernel(slabs, near_ref, local_ref, f_ref, base_ref, nf_hbm, out_ref, n_buf, grad, sums, sem):
    pairs = n_buf.shape[1]
    per = pairs // CHUNKS
    slab = lax.axis_index("mesh")
    mine = lax.axis_index("field")
    masks = lane_masks()

    planes = [(0, 1), (0, 0), (1, 0), (2, 0), (3, 0), (3, 1)]
    for q in range(PLANES):
        for a in range(3):
            before, centre, after = (near_ref[d, e, a] for d, e in planes[q : q + 3])
            slopes = ((after - before) * 0.5, slope_y(centre, masks), slope_z(centre, masks))
            for c in range(3):
                value = slopes[c] * TIME_STEP
                grad[3 * a + c, pl.ds(q, 8, stride=8), :] = value
                grad[3 * a + c, pl.ds(q + 4, 8, stride=8), :] = value

    for ch in range(CHUNKS):

        def block(j, carry):
            rows = pl.ds(pl.multiple_of(8 * j, 8), 8)
            lanes = pl.ds(pl.multiple_of(128 * j, 128), 128)
            g = [grad[k, rows, :] for k in range(9)]
            if ch:
                acc = [sums[k, rows, :] for k in range(6)]
            else:
                acc = [jnp.zeros((8, 128), f32) for _ in range(6)]
            for u in range(per):
                n = ch * per + u
                f = [f_ref[c, n, :, lanes].astype(f32) for c in range(3)]
                a = [
                    base_ref[o, n, :, lanes] + (g[3 * o] * f[0] + g[3 * o + 1] * f[1] + g[3 * o + 2] * f[2])
                    for o in range(3)
                ]
                for c in range(3):
                    n_buf[c, n, :, lanes] = a[c].astype(bf16)
                s = [x * x for x in a]
                r = pltpu.reciprocal(MAX_STRETCH - (s[0] + s[1] + s[2]))
                p0 = r * a[0]
                p1 = r * a[1]
                products = (r * s[0], p0 * a[1], p0 * a[2], r * s[1], p1 * a[2], r * s[2])
                acc = [x + y for x, y in zip(acc, products)]
            for k in range(6):
                sums[k, rows, :] = acc[k]
            return carry

        lax.fori_loop(0, 8, block, 0)
        for copy in stores(ch, n_buf, nf_hbm, sem):
            copy.start()

    scale = VISCOSITY / WEISSENBERG / NF * MAX_STRETCH
    stress = []
    for k in range(6):
        rows = []
        for q in range(PLANES):
            total = sums[k, pl.ds(q, 8, stride=8), :] + sums[k, pl.ds(q + 4, 8, stride=8), :]
            total = total * scale
            if k in DIAGONAL_PAIRS:
                total = total - VISCOSITY / WEISSENBERG / 4
            rows.append(total)
        stress.append(rows)

    own = [mine == q for q in range(PLANES)]
    zero = jnp.zeros((8, 128), f32)
    pressure = [jnp.where(own[q], local_ref[3], 0.0) for q in range(PLANES)]
    start = [[jnp.where(own[q], local_ref[a], 0.0) for q in range(PLANES)] for a in range(3)]

    def at(values, q):
        return values[q] if 0 <= q < PLANES else None

    def add(x, y):
        return y if x is None else x if y is None else x + y

    def halfway(values, q):
        plus, minus = at(values, q + 1), at(values, q - 1)
        if plus is None:
            return None if minus is None else minus * -0.5
        return plus * 0.5 if minus is None else (plus - minus) * 0.5

    first = -(SWEEPS)
    count = PLANES + 2 * SWEEPS
    fluid = []
    for q in range(first, first + count):
        plane = slab * PLANES + q
        inside = (plane >= 0) & (plane < slabs * PLANES)
        wide = plane < slabs * PLANES // 2
        value = jnp.where(masks["channel"] | wide, 1.0 / DIAGONAL, 0.0)
        fluid.append(jnp.where(inside, value, 0.0))

    for a in range(3):
        source = {}
        for q in range(-1, PLANES + 1):
            total = halfway(stress[INDEX[a][0]], q)
            if a == 0:
                total = total - halfway(pressure, q) if total is not None else None
            if 0 <= q < PLANES:
                inner = slope_y(stress[INDEX[a][1]][q], masks) + slope_z(stress[INDEX[a][2]][q], masks)
                if a == 1:
                    inner = inner - slope_y(pressure[q], masks)
                if a == 2:
                    inner = inner - slope_z(pressure[q], masks)
                total = total + inner + start[a][q] * (1.0 / TIME_STEP)
            source[q] = total
        current = {q: start[a][q] for q in range(PLANES)}
        for sweep in range(SWEEPS):
            later = {}
            for q in range(-1 - sweep, PLANES + 1 + sweep):
                total = source.get(q)
                along = add(current.get(q - 1), current.get(q + 1))
                if along is not None:
                    total = add(total, AXIAL * along)
                if q in current:
                    total = add(total, TRANSVERSE * around(current[q], masks))
                later[q] = total * fluid[q - first]
            current = later
        for q in range(first, first + count):
            out_ref[q - first, a] = current[q]

    for ch in range(CHUNKS):
        for copy in stores(ch, n_buf, nf_hbm, sem):
            copy.wait()


def share(near, local, f_flat, base):
    n = f_flat.shape[1]
    slabs = lax.axis_size("mesh")
    vmem = pl.BlockSpec(memory_space=pltpu.VMEM)
    hbm = pl.BlockSpec(memory_space=pl.ANY)
    return pl.pallas_call(
        functools.partial(share_kernel, slabs),
        out_shape=(
            jax.ShapeDtypeStruct((3, n, 2, PLANES, 1024), bf16),
            jax.ShapeDtypeStruct((PLANES + 2 * SWEEPS, 3, 8, 128), f32),
        ),
        in_specs=[vmem] * 4,
        out_specs=[hbm, vmem],
        scratch_shapes=[
            pltpu.VMEM((3, n, 8, 1024), bf16),
            pltpu.VMEM((9, 64, 128), f32),
            pltpu.VMEM((6, 64, 128), f32),
            pltpu.SemaphoreType.DMA((CHUNKS, 6)),
        ],
        compiler_params=pltpu.CompilerParams(vmem_limit_bytes=24 << 20),
    )(near, local, f_flat, base)


def body(velocity, pressure, fields, brownian):
    total = lax.axis_size("mesh") * 4
    mine = lax.axis_index("field")
    low = mine < 2
    core = mine % 2
    cores = [[i, i + 1] for i in range(0, total, 2)]
    inner = [[i, i + 2] for s in range(0, total, 4) for i in (s, s + 1)]

    def gather(x, groups):
        return lax.all_gather(x, AXES, axis=0, axis_index_groups=groups)

    def other(x, first):
        return jnp.where(first, x[1], x[0])

    own = velocity.reshape(3, 8, 128)
    faces = [(i, i + 1) for i in range(3, total - 1, 4)]
    edge = lax.ppermute(own, AXES, faces + [(b, a) for a, b in faces])
    f_flat, base, local = relax(own, pressure.reshape(8, 128), fields, brownian)
    near = lax.all_gather(jnp.stack([own, edge]), "field", axis=0)
    new_fields, shares = share(near, local, f_flat, base)

    both = gather(shares, cores).reshape(2, 3, 2, 2, 3, 8, 128)
    chip = both[0] + both[1]
    chip = jnp.where(core == 0, chip[:, :, 0], chip[:, :, 1])
    low_side = jnp.stack([chip[1, 0], chip[0, 0], chip[0, 1]])
    high_side = jnp.stack([chip[1, 1], chip[2, 0], chip[2, 1]])
    kept = jnp.where(low, low_side, high_side)
    kept = kept + other(gather(jnp.where(low, high_side, low_side), inner), low)
    far = [(i, i + 4) for i in range(total - 4) if i % 4 > 1] + [(i, i - 4) for i in range(4, total) if i % 4 < 2]
    next_to = [(i, i + 2) for i in range(total - 2) if i % 4 > 1] + [(i, i - 2) for i in range(2, total) if i % 4 < 2]
    from_far = lax.ppermute(jnp.where(low, kept[1], kept[2]), AXES, far)
    from_next = lax.ppermute(jnp.where(low, kept[2], kept[1]), AXES, next_to)
    result = kept[0] + (from_far + from_next)
    return new_fields.reshape(fields.shape), result.reshape(velocity.shape)


def solution(mesh):
    placed = (
        P(None, ("mesh", "field"), None),
        P(("mesh", "field"), None),
        P(None, "field", "mesh", None),
        P(None, "field", "mesh", None),
    )
    return jax.shard_map(
        body,
        mesh=mesh,
        in_specs=placed,
        out_specs=(P(None, "field", "mesh", None), P(None, ("mesh", "field"), None)),
        check_vma=False,
    )
```

```python
import functools

import jax
import jax.numpy as jnp
from jax import lax
from jax.experimental import pallas as pl
from jax.experimental.pallas import tpu as pltpu
from jax.sharding import PartitionSpec as P

f32 = jnp.float32
bf16 = jnp.bfloat16

NF = 256
TIME_STEP = 0.02
AXIAL = 400.0
TRANSVERSE = 40.0
MAX_STRETCH = 50.0
VISCOSITY = 40.0
WEISSENBERG = 0.5
NOISE = (0.02 / 0.5) ** 0.5
DIAGONAL = 1.0 / 0.02 + 2.0 * 400.0 + 4.0 * 40.0
SWEEPS = 4
INDEX = ((0, 1, 2), (1, 3, 4), (2, 4, 5))
DIAGONAL_PAIRS = (0, 3, 5)

PLANES = 4
CHUNKS = 4
AXES = ("mesh", "field")


def lane_masks():
    lane = lax.broadcasted_iota(jnp.int32, (8, 128), 1)
    row = lax.broadcasted_iota(jnp.int32, (8, 128), 0)
    return dict(
        z_hi=(lane % 32) < 31,
        z_lo=(lane % 32) > 0,
        lane_hi=lane < 96,
        lane_lo=lane >= 32,
        row_hi=row < 7,
        row_lo=row > 0,
        channel=(row >= 2) & (row < 6),
    )


def shift_z(v, masks):
    plus = jnp.where(masks["z_hi"], pltpu.roll(v, 127, 1), 0.0)
    minus = jnp.where(masks["z_lo"], pltpu.roll(v, 1, 1), 0.0)
    return plus, minus


def shift_y(v, masks):
    ahead = pltpu.roll(v, 96, 1)
    behind = pltpu.roll(v, 32, 1)
    next_row = jnp.where(masks["row_hi"], pltpu.roll(ahead, 7, 0), 0.0)
    last_row = jnp.where(masks["row_lo"], pltpu.roll(behind, 1, 0), 0.0)
    return jnp.where(masks["lane_hi"], ahead, next_row), jnp.where(masks["lane_lo"], behind, last_row)


def slope_y(v, masks):
    plus, minus = shift_y(v, masks)
    return (plus - minus) * 0.5


def slope_z(v, masks):
    plus, minus = shift_z(v, masks)
    return (plus - minus) * 0.5


def around(v, masks):
    y_plus, y_minus = shift_y(v, masks)
    z_plus, z_minus = shift_z(v, masks)
    return (y_plus + y_minus) + (z_plus + z_minus)


def chunk(ch, pairs):
    per = pairs // CHUNKS
    return pl.ds(ch * per, per)


def loads(ch, sources, buffers, sem):
    some = chunk(ch, buffers[0].shape[1])
    return [
        pltpu.make_async_copy(src.at[c, some, h], buf.at[c, some, pl.ds(4 * h, 4), :], sem.at[ch, 6 * w + 2 * c + h])
        for w, (src, buf) in enumerate(zip(sources, buffers))
        for c in range(3)
        for h in range(2)
    ]


def stores(ch, buf, dst, sem):
    some = chunk(ch, buf.shape[1])
    return [
        pltpu.make_async_copy(buf.at[c, some, pl.ds(4 * h, 4), :], dst.at[c, some, h], sem.at[ch, 2 * c + h])
        for c in range(3)
        for h in range(2)
    ]


def relax_kernel(velocity_hbm, pressure_hbm, f_hbm, b_hbm, f_ref, base_ref, local_ref, b_buf, sem, local_sem):
    pairs = b_buf.shape[1]
    per = pairs // CHUNKS
    for ch in range(CHUNKS):
        for copy in loads(ch, (f_hbm, b_hbm), (f_ref, b_buf), sem):
            copy.start()
    own = (
        pltpu.make_async_copy(velocity_hbm, local_ref.at[pl.ds(0, 3)], local_sem.at[0]),
        pltpu.make_async_copy(pressure_hbm, local_ref.at[pl.ds(3, 1)], local_sem.at[1]),
    )
    for copy in own:
        copy.start()
    for ch in range(CHUNKS):
        for copy in loads(ch, (f_hbm, b_hbm), (f_ref, b_buf), sem):
            copy.wait()

        def block(j, carry):
            lanes = pl.ds(pl.multiple_of(128 * j, 128), 128)
            for u in range(per):
                n = ch * per + u
                f = [f_ref[c, n, :, lanes].astype(f32) for c in range(3)]
                length_sq = f[0] * f[0] + f[1] * f[1] + f[2] * f[2]
                pull = TIME_STEP * MAX_STRETCH / (2.0 * WEISSENBERG) * pltpu.reciprocal(MAX_STRETCH - length_sq)
                kept = 1.0 - pull
                for c in range(3):
                    base_ref[c, n, :, lanes] = kept * f[c] + NOISE * b_buf[c, n, :, lanes].astype(f32)
            return carry

        lax.fori_loop(0, 8, block, 0)
    for copy in own:
        copy.wait()


def in_hbm(x):
    return pltpu.with_memory_space_constraint(x, pltpu.HBM)


def relax(velocity, pressure, fields, brownian):
    n = fields.shape[1] // 2
    split = (3, n, 2, PLANES, 1024)
    flat = (3, n, 8, 1024)
    vmem = pl.BlockSpec(memory_space=pltpu.VMEM)
    hbm = pl.BlockSpec(memory_space=pl.ANY)
    return pl.pallas_call(
        relax_kernel,
        out_shape=(
            jax.ShapeDtypeStruct(flat, bf16),
            jax.ShapeDtypeStruct(flat, f32),
            jax.ShapeDtypeStruct((4, 8, 128), f32),
        ),
        in_specs=[hbm] * 4,
        out_specs=[vmem, vmem, vmem],
        scratch_shapes=[
            pltpu.VMEM(flat, bf16),
            pltpu.SemaphoreType.DMA((CHUNKS, 12)),
            pltpu.SemaphoreType.DMA((2,)),
        ],
        compiler_params=pltpu.CompilerParams(vmem_limit_bytes=24 << 20),
        cost_estimate=pl.CostEstimate(flops=10_000_000, bytes_accessed=8_000_000, transcendentals=0),
    )(*(in_hbm(x) for x in (velocity, pressure, fields.reshape(split), brownian.reshape(split))))


def stretch(f, base, g):
    return [base[o] + (g[3 * o] * f[0] + g[3 * o + 1] * f[1] + g[3 * o + 2] * f[2]) for o in range(3)]


def share_kernel(slabs, near_ref, local_ref, f_ref, base_ref, out_ref, grad, sums):
    pairs = f_ref.shape[1]
    per = pairs // CHUNKS
    slab = lax.axis_index("mesh")
    mine = lax.axis_index("field")
    masks = lane_masks()

    planes = [(0, 1), (0, 0), (1, 0), (2, 0), (3, 0), (3, 1)]
    for q in range(PLANES):
        for a in range(3):
            before, centre, after = (near_ref[d, e, a] for d, e in planes[q : q + 3])
            slopes = ((after - before) * 0.5, slope_y(centre, masks), slope_z(centre, masks))
            for c in range(3):
                value = slopes[c] * TIME_STEP
                grad[3 * a + c, pl.ds(q, 8, stride=8), :] = value
                grad[3 * a + c, pl.ds(q + 4, 8, stride=8), :] = value

    for ch in range(CHUNKS):

        def block(j, carry):
            rows = pl.ds(pl.multiple_of(8 * j, 8), 8)
            lanes = pl.ds(pl.multiple_of(128 * j, 128), 128)
            g = [grad[k, rows, :] for k in range(9)]
            if ch:
                acc = [sums[k, rows, :] for k in range(6)]
            else:
                acc = [jnp.zeros((8, 128), f32) for _ in range(6)]
            for u in range(per):
                n = ch * per + u
                f = [f_ref[c, n, :, lanes].astype(f32) for c in range(3)]
                a = stretch(f, [base_ref[o, n, :, lanes] for o in range(3)], g)
                s = [x * x for x in a]
                r = pltpu.reciprocal(MAX_STRETCH - (s[0] + s[1] + s[2]))
                p0 = r * a[0]
                p1 = r * a[1]
                products = (r * s[0], p0 * a[1], p0 * a[2], r * s[1], p1 * a[2], r * s[2])
                acc = [x + y for x, y in zip(acc, products)]
            for k in range(6):
                sums[k, rows, :] = acc[k]
            return carry

        lax.fori_loop(0, 8, block, 0)

    scale = VISCOSITY / WEISSENBERG / NF * MAX_STRETCH
    stress = []
    for k in range(6):
        rows = []
        for q in range(PLANES):
            total = sums[k, pl.ds(q, 8, stride=8), :] + sums[k, pl.ds(q + 4, 8, stride=8), :]
            total = total * scale
            if k in DIAGONAL_PAIRS:
                total = total - VISCOSITY / WEISSENBERG / 4
            rows.append(total)
        stress.append(rows)

    own = [mine == q for q in range(PLANES)]
    zero = jnp.zeros((8, 128), f32)
    pressure = [jnp.where(own[q], local_ref[3], 0.0) for q in range(PLANES)]
    start = [[jnp.where(own[q], local_ref[a], 0.0) for q in range(PLANES)] for a in range(3)]

    def at(values, q):
        return values[q] if 0 <= q < PLANES else None

    def add(x, y):
        return y if x is None else x if y is None else x + y

    def halfway(values, q):
        plus, minus = at(values, q + 1), at(values, q - 1)
        if plus is None:
            return None if minus is None else minus * -0.5
        return plus * 0.5 if minus is None else (plus - minus) * 0.5

    first = -(SWEEPS)
    count = PLANES + 2 * SWEEPS
    fluid = []
    for q in range(first, first + count):
        plane = slab * PLANES + q
        inside = (plane >= 0) & (plane < slabs * PLANES)
        wide = plane < slabs * PLANES // 2
        value = jnp.where(masks["channel"] | wide, 1.0 / DIAGONAL, 0.0)
        fluid.append(jnp.where(inside, value, 0.0))

    for a in range(3):
        source = {}
        for q in range(-1, PLANES + 1):
            total = halfway(stress[INDEX[a][0]], q)
            if a == 0:
                total = total - halfway(pressure, q) if total is not None else None
            if 0 <= q < PLANES:
                inner = slope_y(stress[INDEX[a][1]][q], masks) + slope_z(stress[INDEX[a][2]][q], masks)
                if a == 1:
                    inner = inner - slope_y(pressure[q], masks)
                if a == 2:
                    inner = inner - slope_z(pressure[q], masks)
                total = total + inner + start[a][q] * (1.0 / TIME_STEP)
            source[q] = total
        current = {q: start[a][q] for q in range(PLANES)}
        for sweep in range(SWEEPS):
            later = {}
            for q in range(-1 - sweep, PLANES + 1 + sweep):
                total = source.get(q)
                along = add(current.get(q - 1), current.get(q + 1))
                if along is not None:
                    total = add(total, AXIAL * along)
                if q in current:
                    total = add(total, TRANSVERSE * around(current[q], masks))
                later[q] = total * fluid[q - first]
            current = later
        for q in range(first, first + count):
            out_ref[q - first, a] = current[q]


def share(near, local, f_flat, base):
    slabs = lax.axis_size("mesh")
    vmem = pl.BlockSpec(memory_space=pltpu.VMEM)
    return pl.pallas_call(
        functools.partial(share_kernel, slabs),
        out_shape=(
            jax.ShapeDtypeStruct((PLANES + 2 * SWEEPS, 3, 8, 128), f32),
            jax.ShapeDtypeStruct((9, 64, 128), f32),
        ),
        in_specs=[vmem] * 4,
        out_specs=[vmem] * 2,
        scratch_shapes=[pltpu.VMEM((6, 64, 128), f32)],
        compiler_params=pltpu.CompilerParams(vmem_limit_bytes=16 << 20),
        cost_estimate=pl.CostEstimate(flops=12_000_000, bytes_accessed=5_000_000, transcendentals=0),
    )(near, local, f_flat, base)


def advance_kernel(grad, f_ref, base_ref, nf_hbm, n_buf, sem):
    pairs = n_buf.shape[1]
    per = pairs // CHUNKS
    for ch in range(CHUNKS):

        def block(j, carry):
            rows = pl.ds(pl.multiple_of(8 * j, 8), 8)
            lanes = pl.ds(pl.multiple_of(128 * j, 128), 128)
            g = [grad[k, rows, :] for k in range(9)]
            for u in range(per):
                n = ch * per + u
                f = [f_ref[c, n, :, lanes].astype(f32) for c in range(3)]
                a = stretch(f, [base_ref[o, n, :, lanes] for o in range(3)], g)
                for c in range(3):
                    n_buf[c, n, :, lanes] = a[c].astype(bf16)
            return carry

        lax.fori_loop(0, 8, block, 0)
        for copy in stores(ch, n_buf, nf_hbm, sem):
            copy.start()
    for ch in range(CHUNKS):
        for copy in stores(ch, n_buf, nf_hbm, sem):
            copy.wait()


def advance(grad, f_flat, base):
    n = f_flat.shape[1]
    vmem = pl.BlockSpec(memory_space=pltpu.VMEM)
    return pl.pallas_call(
        advance_kernel,
        out_shape=jax.ShapeDtypeStruct((3, n, 2, PLANES, 1024), bf16),
        in_specs=[vmem] * 3,
        out_specs=pl.BlockSpec(memory_space=pl.ANY),
        scratch_shapes=[pltpu.VMEM((3, n, 8, 1024), bf16), pltpu.SemaphoreType.DMA((CHUNKS, 6))],
        compiler_params=pltpu.CompilerParams(vmem_limit_bytes=16 << 20),
        cost_estimate=pl.CostEstimate(flops=6_000_000, bytes_accessed=6_000_000, transcendentals=0),
    )(grad, f_flat, base)


def body(velocity, pressure, fields, brownian):
    total = lax.axis_size("mesh") * 4
    mine = lax.axis_index("field")
    low = mine < 2
    core = mine % 2
    cores = [[i, i + 1] for i in range(0, total, 2)]
    inner = [[i, i + 2] for s in range(0, total, 4) for i in (s, s + 1)]

    def gather(x, groups):
        return lax.all_gather(x, AXES, axis=0, axis_index_groups=groups)

    def other(x, first):
        return jnp.where(first, x[1], x[0])

    own = velocity.reshape(3, 8, 128)
    faces = [(i, i + 1) for i in range(3, total - 1, 4)]
    edge = lax.ppermute(own, AXES, faces + [(b, a) for a, b in faces])
    f_flat, base, local = relax(own, pressure.reshape(1, 8, 128), fields, brownian)
    near = lax.all_gather(jnp.stack([own, edge]), "field", axis=0)
    shares, grad = share(near, local, f_flat, base)

    both = gather(shares, cores).reshape(2, 3, 2, 2, 3, 8, 128)
    chip = both[0] + both[1]
    chip = jnp.where(core == 0, chip[:, :, 0], chip[:, :, 1])
    low_side = jnp.stack([chip[1, 0], chip[0, 0], chip[0, 1]])
    high_side = jnp.stack([chip[1, 1], chip[2, 0], chip[2, 1]])
    kept = jnp.where(low, low_side, high_side)
    kept = kept + other(gather(jnp.where(low, high_side, low_side), inner), low)
    next_to = [(i, i + 2) for i in range(total - 2) if i % 4 > 1]
    arrived = lax.ppermute(kept[1:], AXES, next_to + [(b, a) for a, b in next_to])
    new_fields = advance(grad, f_flat, base)
    passed = jnp.where(low, arrived[1], arrived[0])
    result = kept[0] + jnp.where(low, arrived[0], arrived[1]) + other(gather(passed, inner), low)
    return new_fields.reshape(fields.shape), result.reshape(velocity.shape)


def solution(mesh):
    placed = (
        P(None, ("mesh", "field"), None),
        P(("mesh", "field"), None),
        P(None, "field", "mesh", None),
        P(None, "field", "mesh", None),
    )
    return jax.shard_map(
        body,
        mesh=mesh,
        in_specs=placed,
        out_specs=(P(None, "field", "mesh", None), P(None, ("mesh", "field"), None)),
        check_vma=False,
    )
```

```python
import functools

import jax
import jax.numpy as jnp
from jax import lax
from jax.experimental import pallas as pl
from jax.experimental.pallas import tpu as pltpu
from jax.sharding import PartitionSpec as P

f32 = jnp.float32
bf16 = jnp.bfloat16

NF = 256
TIME_STEP = 0.02
AXIAL = 400.0
TRANSVERSE = 40.0
MAX_STRETCH = 50.0
VISCOSITY = 40.0
WEISSENBERG = 0.5
NOISE = (0.02 / 0.5) ** 0.5
DIAGONAL = 1.0 / 0.02 + 2.0 * 400.0 + 4.0 * 40.0
SWEEPS = 4
INDEX = ((0, 1, 2), (1, 3, 4), (2, 4, 5))
DIAGONAL_PAIRS = (0, 3, 5)

PLANES = 4
CHUNKS = 4
AXES = ("mesh", "field")


def lane_masks():
    lane = lax.broadcasted_iota(jnp.int32, (8, 128), 1)
    row = lax.broadcasted_iota(jnp.int32, (8, 128), 0)
    return dict(
        z_hi=(lane % 32) < 31,
        z_lo=(lane % 32) > 0,
        lane_hi=lane < 96,
        lane_lo=lane >= 32,
        row_hi=row < 7,
        row_lo=row > 0,
        channel=(row >= 2) & (row < 6),
    )


def shift_z(v, masks):
    plus = jnp.where(masks["z_hi"], pltpu.roll(v, 127, 1), 0.0)
    minus = jnp.where(masks["z_lo"], pltpu.roll(v, 1, 1), 0.0)
    return plus, minus


def shift_y(v, masks):
    ahead = pltpu.roll(v, 96, 1)
    behind = pltpu.roll(v, 32, 1)
    next_row = jnp.where(masks["row_hi"], pltpu.roll(ahead, 7, 0), 0.0)
    last_row = jnp.where(masks["row_lo"], pltpu.roll(behind, 1, 0), 0.0)
    return jnp.where(masks["lane_hi"], ahead, next_row), jnp.where(masks["lane_lo"], behind, last_row)


def slope_y(v, masks):
    plus, minus = shift_y(v, masks)
    return (plus - minus) * 0.5


def slope_z(v, masks):
    plus, minus = shift_z(v, masks)
    return (plus - minus) * 0.5


def around(v, masks):
    y_plus, y_minus = shift_y(v, masks)
    z_plus, z_minus = shift_z(v, masks)
    return (y_plus + y_minus) + (z_plus + z_minus)


def chunk(ch, pairs):
    per = pairs // CHUNKS
    return pl.ds(ch * per, per)


def loads(ch, sources, buffers, sem):
    some = chunk(ch, buffers[0].shape[1])
    return [
        pltpu.make_async_copy(src.at[c, some, h], buf.at[c, some, pl.ds(4 * h, 4), :], sem.at[ch, 6 * w + 2 * c + h])
        for w, (src, buf) in enumerate(zip(sources, buffers))
        for c in range(3)
        for h in range(2)
    ]


def stores(ch, buf, dst, sem):
    some = chunk(ch, buf.shape[1])
    return [
        pltpu.make_async_copy(buf.at[c, some, pl.ds(4 * h, 4), :], dst.at[c, some, h], sem.at[ch, 2 * c + h])
        for c in range(3)
        for h in range(2)
    ]


def relax_kernel(velocity_hbm, pressure_hbm, f_hbm, b_hbm, f_ref, base_ref, local_ref, b_buf, sem, local_sem):
    pairs = b_buf.shape[1]
    per = pairs // CHUNKS
    for ch in range(CHUNKS):
        for copy in loads(ch, (f_hbm, b_hbm), (f_ref, b_buf), sem):
            copy.start()
    own = (
        pltpu.make_async_copy(velocity_hbm, local_ref.at[pl.ds(0, 3)], local_sem.at[0]),
        pltpu.make_async_copy(pressure_hbm, local_ref.at[pl.ds(3, 1)], local_sem.at[1]),
    )
    for copy in own:
        copy.start()
    for ch in range(CHUNKS):
        for copy in loads(ch, (f_hbm, b_hbm), (f_ref, b_buf), sem):
            copy.wait()

        def block(j, carry):
            lanes = pl.ds(pl.multiple_of(128 * j, 128), 128)
            for u in range(per):
                n = ch * per + u
                f = [f_ref[c, n, :, lanes].astype(f32) for c in range(3)]
                length_sq = f[0] * f[0] + f[1] * f[1] + f[2] * f[2]
                pull = TIME_STEP * MAX_STRETCH / (2.0 * WEISSENBERG) * pltpu.reciprocal(MAX_STRETCH - length_sq)
                kept = 1.0 - pull
                for c in range(3):
                    base_ref[c, n, :, lanes] = kept * f[c] + NOISE * b_buf[c, n, :, lanes].astype(f32)
            return carry

        lax.fori_loop(0, 8, block, 0)
    for copy in own:
        copy.wait()


def in_hbm(x):
    return pltpu.with_memory_space_constraint(x, pltpu.HBM)


def relax(velocity, pressure, fields, brownian):
    n = fields.shape[1] // 2
    split = (3, n, 2, PLANES, 1024)
    flat = (3, n, 8, 1024)
    vmem = pl.BlockSpec(memory_space=pltpu.VMEM)
    hbm = pl.BlockSpec(memory_space=pl.ANY)
    return pl.pallas_call(
        relax_kernel,
        out_shape=(
            jax.ShapeDtypeStruct(flat, bf16),
            jax.ShapeDtypeStruct(flat, f32),
            jax.ShapeDtypeStruct((4, 8, 128), f32),
        ),
        in_specs=[hbm] * 4,
        out_specs=[vmem, vmem, vmem],
        scratch_shapes=[
            pltpu.VMEM(flat, bf16),
            pltpu.SemaphoreType.DMA((CHUNKS, 12)),
            pltpu.SemaphoreType.DMA((2,)),
        ],
        compiler_params=pltpu.CompilerParams(vmem_limit_bytes=24 << 20),
        cost_estimate=pl.CostEstimate(flops=10_000_000, bytes_accessed=8_000_000, transcendentals=0),
    )(*(in_hbm(x) for x in (velocity, pressure, fields.reshape(split), brownian.reshape(split))))


def stretch(f, base, g):
    return [base[o] + (g[3 * o] * f[0] + g[3 * o + 1] * f[1] + g[3 * o + 2] * f[2]) for o in range(3)]


def share_kernel(slabs, near_ref, local_ref, f_ref, base_ref, own_ref, outer_ref, inner_ref, grad, sums):
    pairs = f_ref.shape[1]
    per = pairs // CHUNKS
    slab = lax.axis_index("mesh")
    mine = lax.axis_index("field")
    masks = lane_masks()

    planes = [(0, 1), (0, 0), (1, 0), (2, 0), (3, 0), (3, 1)]
    for q in range(PLANES):
        for a in range(3):
            before, centre, after = (near_ref[d, e, a] for d, e in planes[q : q + 3])
            slopes = ((after - before) * 0.5, slope_y(centre, masks), slope_z(centre, masks))
            for c in range(3):
                value = slopes[c] * TIME_STEP
                grad[3 * a + c, pl.ds(q, 8, stride=8), :] = value
                grad[3 * a + c, pl.ds(q + 4, 8, stride=8), :] = value

    for ch in range(CHUNKS):

        def block(j, carry):
            rows = pl.ds(pl.multiple_of(8 * j, 8), 8)
            lanes = pl.ds(pl.multiple_of(128 * j, 128), 128)
            g = [grad[k, rows, :] for k in range(9)]
            if ch:
                acc = [sums[k, rows, :] for k in range(6)]
            else:
                acc = [jnp.zeros((8, 128), f32) for _ in range(6)]
            for u in range(per):
                n = ch * per + u
                f = [f_ref[c, n, :, lanes].astype(f32) for c in range(3)]
                a = stretch(f, [base_ref[o, n, :, lanes] for o in range(3)], g)
                s = [x * x for x in a]
                r = pltpu.reciprocal(MAX_STRETCH - (s[0] + s[1] + s[2]))
                p0 = r * a[0]
                p1 = r * a[1]
                products = (r * s[0], p0 * a[1], p0 * a[2], r * s[1], p1 * a[2], r * s[2])
                acc = [x + y for x, y in zip(acc, products)]
            for k in range(6):
                sums[k, rows, :] = acc[k]
            return carry

        lax.fori_loop(0, 8, block, 0)

    scale = VISCOSITY / WEISSENBERG / NF * MAX_STRETCH
    stress = []
    for k in range(6):
        rows = []
        for q in range(PLANES):
            total = sums[k, pl.ds(q, 8, stride=8), :] + sums[k, pl.ds(q + 4, 8, stride=8), :]
            total = total * scale
            if k in DIAGONAL_PAIRS:
                total = total - VISCOSITY / WEISSENBERG / 4
            rows.append(total)
        stress.append(rows)

    own = [mine == q for q in range(PLANES)]
    zero = jnp.zeros((8, 128), f32)
    pressure = [jnp.where(own[q], local_ref[3], 0.0) for q in range(PLANES)]
    start = [[jnp.where(own[q], local_ref[a], 0.0) for q in range(PLANES)] for a in range(3)]

    def at(values, q):
        return values[q] if 0 <= q < PLANES else None

    def add(x, y):
        return y if x is None else x if y is None else x + y

    def halfway(values, q):
        plus, minus = at(values, q + 1), at(values, q - 1)
        if plus is None:
            return None if minus is None else minus * -0.5
        return plus * 0.5 if minus is None else (plus - minus) * 0.5

    first = -(SWEEPS)
    count = PLANES + 2 * SWEEPS
    fluid = []
    for q in range(first, first + count):
        plane = slab * PLANES + q
        inside = (plane >= 0) & (plane < slabs * PLANES)
        wide = plane < slabs * PLANES // 2
        value = jnp.where(masks["channel"] | wide, 1.0 / DIAGONAL, 0.0)
        fluid.append(jnp.where(inside, value, 0.0))

    for a in range(3):
        source = {}
        for q in range(-1, PLANES + 1):
            total = halfway(stress[INDEX[a][0]], q)
            if a == 0:
                total = total - halfway(pressure, q) if total is not None else None
            if 0 <= q < PLANES:
                inner = slope_y(stress[INDEX[a][1]][q], masks) + slope_z(stress[INDEX[a][2]][q], masks)
                if a == 1:
                    inner = inner - slope_y(pressure[q], masks)
                if a == 2:
                    inner = inner - slope_z(pressure[q], masks)
                total = total + inner + start[a][q] * (1.0 / TIME_STEP)
            source[q] = total
        current = {q: start[a][q] for q in range(PLANES)}
        for sweep in range(SWEEPS):
            later = {}
            for q in range(-1 - sweep, PLANES + 1 + sweep):
                total = source.get(q)
                along = add(current.get(q - 1), current.get(q + 1))
                if along is not None:
                    total = add(total, AXIAL * along)
                if q in current:
                    total = add(total, TRANSVERSE * around(current[q], masks))
                later[q] = total * fluid[q - first]
            current = later
        odd = slab % 2 == 1
        for q in range(PLANES):
            before, after = current[q - PLANES], current[q + PLANES]
            own_ref[q, a] = current[q]
            outer_ref[q, a] = jnp.where(odd, after, before)
            inner_ref[q, a] = jnp.where(odd, before, after)


def share(near, local, f_flat, base):
    slabs = lax.axis_size("mesh")
    vmem = pl.BlockSpec(memory_space=pltpu.VMEM)
    return pl.pallas_call(
        functools.partial(share_kernel, slabs),
        out_shape=(
            jax.ShapeDtypeStruct((PLANES, 3, 8, 128), f32),
            jax.ShapeDtypeStruct((PLANES, 3, 8, 128), f32),
            jax.ShapeDtypeStruct((PLANES, 3, 8, 128), f32),
            jax.ShapeDtypeStruct((9, 64, 128), f32),
        ),
        in_specs=[vmem] * 4,
        out_specs=[vmem] * 4,
        scratch_shapes=[pltpu.VMEM((6, 64, 128), f32)],
        compiler_params=pltpu.CompilerParams(vmem_limit_bytes=16 << 20),
        cost_estimate=pl.CostEstimate(flops=12_000_000, bytes_accessed=5_000_000, transcendentals=0),
    )(near, local, f_flat, base)


def advance_kernel(grad, f_ref, base_ref, nf_hbm, n_buf, sem):
    pairs = n_buf.shape[1]
    per = pairs // CHUNKS
    for ch in range(CHUNKS):

        def block(j, carry):
            rows = pl.ds(pl.multiple_of(8 * j, 8), 8)
            lanes = pl.ds(pl.multiple_of(128 * j, 128), 128)
            g = [grad[k, rows, :] for k in range(9)]
            for u in range(per):
                n = ch * per + u
                f = [f_ref[c, n, :, lanes].astype(f32) for c in range(3)]
                a = stretch(f, [base_ref[o, n, :, lanes] for o in range(3)], g)
                for c in range(3):
                    n_buf[c, n, :, lanes] = a[c].astype(bf16)
            return carry

        lax.fori_loop(0, 8, block, 0)
        for copy in stores(ch, n_buf, nf_hbm, sem):
            copy.start()
    for ch in range(CHUNKS):
        for copy in stores(ch, n_buf, nf_hbm, sem):
            copy.wait()


def advance(grad, f_flat, base):
    n = f_flat.shape[1]
    vmem = pl.BlockSpec(memory_space=pltpu.VMEM)
    return pl.pallas_call(
        advance_kernel,
        out_shape=jax.ShapeDtypeStruct((3, n, 2, PLANES, 1024), bf16),
        in_specs=[vmem] * 3,
        out_specs=pl.BlockSpec(memory_space=pl.ANY),
        scratch_shapes=[pltpu.VMEM((3, n, 8, 1024), bf16), pltpu.SemaphoreType.DMA((CHUNKS, 6))],
        compiler_params=pltpu.CompilerParams(vmem_limit_bytes=16 << 20),
        cost_estimate=pl.CostEstimate(flops=6_000_000, bytes_accessed=6_000_000, transcendentals=0),
    )(grad, f_flat, base)


def body(velocity, pressure, fields, brownian):
    total = lax.axis_size("mesh") * PLANES

    def exchange(x, pairs):
        return lax.ppermute(x, AXES, pairs + [(b, a) for a, b in pairs])

    own = velocity.reshape(3, 8, 128)
    edge = exchange(own, [(i, i + 1) for i in range(PLANES - 1, total - 1, PLANES)])
    f_flat, base, local = relax(own, pressure.reshape(1, 8, 128), fields, brownian)
    near = lax.all_gather(jnp.stack([own, edge]), "field", axis=0)
    kept, outer, inner, grad = share(near, local, f_flat, base)

    neighbours = [(i, i + PLANES) for i in range(total - PLANES)]
    outer = exchange(outer, [p for p in neighbours if p[0] // PLANES % 2 == 1])
    inner = exchange(inner, [p for p in neighbours if p[0] // PLANES % 2 == 0])
    kept, new_fields = lax.optimization_barrier((kept, advance(grad, f_flat, base)))
    parts = lax.all_to_all(kept + (outer + inner), "field", 0, 0, tiled=True)
    result = (parts[0] + parts[1]) + (parts[2] + parts[3])
    return new_fields.reshape(fields.shape), result.reshape(velocity.shape)


def solution(mesh):
    placed = (
        P(None, ("mesh", "field"), None),
        P(("mesh", "field"), None),
        P(None, "field", "mesh", None),
        P(None, "field", "mesh", None),
    )
    return jax.shard_map(
        body,
        mesh=mesh,
        in_specs=placed,
        out_specs=(P(None, "field", "mesh", None), P(None, ("mesh", "field"), None)),
        check_vma=False,
    )
```

```python
import functools

import jax
import jax.numpy as jnp
from jax import lax
from jax.experimental import pallas as pl
from jax.experimental.pallas import tpu as pltpu
from jax.sharding import PartitionSpec as P

f32 = jnp.float32
bf16 = jnp.bfloat16

NF = 256
TIME_STEP = 0.02
AXIAL = 400.0
TRANSVERSE = 40.0
MAX_STRETCH = 50.0
VISCOSITY = 40.0
WEISSENBERG = 0.5
NOISE = (0.02 / 0.5) ** 0.5
DIAGONAL = 1.0 / 0.02 + 2.0 * 400.0 + 4.0 * 40.0
SWEEPS = 4
INDEX = ((0, 1, 2), (1, 3, 4), (2, 4, 5))
DIAGONAL_PAIRS = (0, 3, 5)

PLANES = 4
CHUNKS = 4
PARTS = 2
AXES = ("mesh", "field")


def lane_masks():
    lane = lax.broadcasted_iota(jnp.int32, (8, 128), 1)
    row = lax.broadcasted_iota(jnp.int32, (8, 128), 0)
    return dict(
        z_hi=(lane % 32) < 31,
        z_lo=(lane % 32) > 0,
        lane_hi=lane < 96,
        lane_lo=lane >= 32,
        row_hi=row < 7,
        row_lo=row > 0,
        channel=(row >= 2) & (row < 6),
    )


def shift_z(v, masks):
    plus = jnp.where(masks["z_hi"], pltpu.roll(v, 127, 1), 0.0)
    minus = jnp.where(masks["z_lo"], pltpu.roll(v, 1, 1), 0.0)
    return plus, minus


def shift_y(v, masks):
    ahead = pltpu.roll(v, 96, 1)
    behind = pltpu.roll(v, 32, 1)
    next_row = jnp.where(masks["row_hi"], pltpu.roll(ahead, 7, 0), 0.0)
    last_row = jnp.where(masks["row_lo"], pltpu.roll(behind, 1, 0), 0.0)
    return jnp.where(masks["lane_hi"], ahead, next_row), jnp.where(masks["lane_lo"], behind, last_row)


def slope_y(v, masks):
    plus, minus = shift_y(v, masks)
    return (plus - minus) * 0.5


def slope_z(v, masks):
    plus, minus = shift_z(v, masks)
    return (plus - minus) * 0.5


def around(v, masks):
    y_plus, y_minus = shift_y(v, masks)
    z_plus, z_minus = shift_z(v, masks)
    return (y_plus + y_minus) + (z_plus + z_minus)


def chunk(ch, pairs):
    per = pairs // CHUNKS
    return pl.ds(ch * per, per)


def loads(ch, sources, buffers, sem):
    some = chunk(ch, buffers[0].shape[1])
    return [
        pltpu.make_async_copy(src.at[c, some, h], buf.at[c, some, pl.ds(4 * h, 4), :], sem.at[ch, 6 * w + 2 * c + h])
        for w, (src, buf) in enumerate(zip(sources, buffers))
        for c in range(3)
        for h in range(2)
    ]


def stores(ch, buf, dst, sem):
    some = chunk(ch, buf.shape[1])
    return [
        pltpu.make_async_copy(buf.at[c, some, pl.ds(4 * h, 4), :], dst.at[c, some, h], sem.at[ch, 2 * c + h])
        for c in range(3)
        for h in range(2)
    ]


def relax_kernel(velocity_hbm, pressure_hbm, f_hbm, b_hbm, f_ref, base_ref, local_ref, b_buf, sem, local_sem):
    pairs = b_buf.shape[1]
    per = pairs // CHUNKS
    for ch in range(CHUNKS):
        for copy in loads(ch, (f_hbm, b_hbm), (f_ref, b_buf), sem):
            copy.start()
    own = (
        pltpu.make_async_copy(velocity_hbm, local_ref.at[pl.ds(0, 3)], local_sem.at[0]),
        pltpu.make_async_copy(pressure_hbm, local_ref.at[pl.ds(3, 1)], local_sem.at[1]),
    )
    for copy in own:
        copy.start()
    for ch in range(CHUNKS):
        for copy in loads(ch, (f_hbm, b_hbm), (f_ref, b_buf), sem):
            copy.wait()

        def block(j, carry):
            lanes = pl.ds(pl.multiple_of(128 * j, 128), 128)
            for u in range(per):
                n = ch * per + u
                f = [f_ref[c, n, :, lanes].astype(f32) for c in range(3)]
                length_sq = f[0] * f[0] + f[1] * f[1] + f[2] * f[2]
                pull = TIME_STEP * MAX_STRETCH / (2.0 * WEISSENBERG) * pltpu.reciprocal(MAX_STRETCH - length_sq)
                kept = 1.0 - pull
                for c in range(3):
                    base_ref[c, n, :, lanes] = kept * f[c] + NOISE * b_buf[c, n, :, lanes].astype(f32)
            return carry

        lax.fori_loop(0, 8, block, 0)
    for copy in own:
        copy.wait()


def in_hbm(x):
    return pltpu.with_memory_space_constraint(x, pltpu.HBM)


def relax(velocity, pressure, fields, brownian):
    n = fields.shape[1] // 2
    split = (3, n, 2, PLANES, 1024)
    flat = (3, n, 8, 1024)
    vmem = pl.BlockSpec(memory_space=pltpu.VMEM)
    hbm = pl.BlockSpec(memory_space=pl.ANY)
    return pl.pallas_call(
        relax_kernel,
        out_shape=(
            jax.ShapeDtypeStruct(flat, bf16),
            jax.ShapeDtypeStruct(flat, f32),
            jax.ShapeDtypeStruct((4, 8, 128), f32),
        ),
        in_specs=[hbm] * 4,
        out_specs=[vmem, vmem, vmem],
        scratch_shapes=[
            pltpu.VMEM(flat, bf16),
            pltpu.SemaphoreType.DMA((CHUNKS, 12)),
            pltpu.SemaphoreType.DMA((2,)),
        ],
        compiler_params=pltpu.CompilerParams(vmem_limit_bytes=24 << 20),
        cost_estimate=pl.CostEstimate(flops=10_000_000, bytes_accessed=8_000_000, transcendentals=0),
    )(*(in_hbm(x) for x in (velocity, pressure, fields.reshape(split), brownian.reshape(split))))


def stretch(f, base, g):
    return [base[o] + (g[3 * o] * f[0] + g[3 * o + 1] * f[1] + g[3 * o + 2] * f[2]) for o in range(3)]


def share_kernel(slabs, near_ref, local_ref, f_ref, base_ref, own_ref, outer_ref, inner_ref, grad, sums):
    pairs = f_ref.shape[1]
    per = pairs // PARTS
    slab = lax.axis_index("mesh")
    mine = lax.axis_index("field")
    masks = lane_masks()

    planes = [(0, 1), (0, 0), (1, 0), (2, 0), (3, 0), (3, 1)]
    for q in range(PLANES):
        for a in range(3):
            before, centre, after = (near_ref[d, e, a] for d, e in planes[q : q + 3])
            slopes = ((after - before) * 0.5, slope_y(centre, masks), slope_z(centre, masks))
            for c in range(3):
                value = slopes[c] * TIME_STEP
                grad[3 * a + c, pl.ds(q, 8, stride=8), :] = value
                grad[3 * a + c, pl.ds(q + 4, 8, stride=8), :] = value

    for ch in range(PARTS):

        def block(j, carry):
            rows = pl.ds(pl.multiple_of(8 * j, 8), 8)
            lanes = pl.ds(pl.multiple_of(128 * j, 128), 128)
            g = [grad[k, rows, :] for k in range(9)]
            if ch:
                acc = [sums[k, rows, :] for k in range(6)]
            else:
                acc = [jnp.zeros((8, 128), f32) for _ in range(6)]
            for u in range(per):
                n = ch * per + u
                f = [f_ref[c, n, :, lanes].astype(f32) for c in range(3)]
                a = stretch(f, [base_ref[o, n, :, lanes] for o in range(3)], g)
                s = [x * x for x in a]
                r = pltpu.reciprocal(MAX_STRETCH - (s[0] + s[1] + s[2]))
                p0 = r * a[0]
                p1 = r * a[1]
                products = (r * s[0], p0 * a[1], p0 * a[2], r * s[1], p1 * a[2], r * s[2])
                acc = [x + y for x, y in zip(acc, products)]
            for k in range(6):
                sums[k, rows, :] = acc[k]
            return carry

        lax.fori_loop(0, 8, block, 0)

    scale = VISCOSITY / WEISSENBERG / NF * MAX_STRETCH
    stress = []
    for k in range(6):
        rows = []
        for q in range(PLANES):
            total = sums[k, pl.ds(q, 8, stride=8), :] + sums[k, pl.ds(q + 4, 8, stride=8), :]
            total = total * scale
            if k in DIAGONAL_PAIRS:
                total = total - VISCOSITY / WEISSENBERG / 4
            rows.append(total)
        stress.append(rows)

    own = [mine == q for q in range(PLANES)]
    zero = jnp.zeros((8, 128), f32)
    pressure = [jnp.where(own[q], local_ref[3], 0.0) for q in range(PLANES)]
    start = [[jnp.where(own[q], local_ref[a], 0.0) for q in range(PLANES)] for a in range(3)]

    def at(values, q):
        return values[q] if 0 <= q < PLANES else None

    def add(x, y):
        return y if x is None else x if y is None else x + y

    def halfway(values, q):
        plus, minus = at(values, q + 1), at(values, q - 1)
        if plus is None:
            return None if minus is None else minus * -0.5
        return plus * 0.5 if minus is None else (plus - minus) * 0.5

    first = -(SWEEPS)
    count = PLANES + 2 * SWEEPS
    fluid = []
    for q in range(first, first + count):
        plane = slab * PLANES + q
        inside = (plane >= 0) & (plane < slabs * PLANES)
        wide = plane < slabs * PLANES // 2
        value = jnp.where(masks["channel"] | wide, 1.0 / DIAGONAL, 0.0)
        fluid.append(jnp.where(inside, value, 0.0))

    for a in range(3):
        source = {}
        for q in range(-1, PLANES + 1):
            total = halfway(stress[INDEX[a][0]], q)
            if a == 0:
                total = total - halfway(pressure, q) if total is not None else None
            if 0 <= q < PLANES:
                inner = slope_y(stress[INDEX[a][1]][q], masks) + slope_z(stress[INDEX[a][2]][q], masks)
                if a == 1:
                    inner = inner - slope_y(pressure[q], masks)
                if a == 2:
                    inner = inner - slope_z(pressure[q], masks)
                total = total + inner + start[a][q] * (1.0 / TIME_STEP)
            source[q] = total
        current = {q: start[a][q] for q in range(PLANES)}
        for sweep in range(SWEEPS):
            later = {}
            for q in range(-1 - sweep, PLANES + 1 + sweep):
                total = source.get(q)
                along = add(current.get(q - 1), current.get(q + 1))
                if along is not None:
                    total = add(total, AXIAL * along)
                if q in current:
                    total = add(total, TRANSVERSE * around(current[q], masks))
                later[q] = total * fluid[q - first]
            current = later
        odd = slab % 2 == 1
        for q in range(PLANES):
            before, after = current[q - PLANES], current[q + PLANES]
            own_ref[q, a] = current[q]
            outer_ref[q, a] = jnp.where(odd, after, before)
            inner_ref[q, a] = jnp.where(odd, before, after)


def share(near, local, f_flat, base):
    slabs = lax.axis_size("mesh")
    vmem = pl.BlockSpec(memory_space=pltpu.VMEM)
    return pl.pallas_call(
        functools.partial(share_kernel, slabs),
        out_shape=(
            jax.ShapeDtypeStruct((PLANES, 3, 8, 128), f32),
            jax.ShapeDtypeStruct((PLANES, 3, 8, 128), f32),
            jax.ShapeDtypeStruct((PLANES, 3, 8, 128), f32),
            jax.ShapeDtypeStruct((9, 64, 128), f32),
        ),
        in_specs=[vmem] * 4,
        out_specs=[vmem] * 4,
        scratch_shapes=[pltpu.VMEM((6, 64, 128), f32)],
        compiler_params=pltpu.CompilerParams(vmem_limit_bytes=16 << 20),
        cost_estimate=pl.CostEstimate(flops=12_000_000, bytes_accessed=5_000_000, transcendentals=0),
    )(near, local, f_flat, base)


def advance_kernel(grad, f_ref, base_ref, nf_hbm, n_buf, sem):
    pairs = n_buf.shape[1]
    per = pairs // CHUNKS
    for ch in range(CHUNKS):

        def block(j, carry):
            rows = pl.ds(pl.multiple_of(8 * j, 8), 8)
            lanes = pl.ds(pl.multiple_of(128 * j, 128), 128)
            g = [grad[k, rows, :] for k in range(9)]
            for u in range(per):
                n = ch * per + u
                f = [f_ref[c, n, :, lanes].astype(f32) for c in range(3)]
                a = stretch(f, [base_ref[o, n, :, lanes] for o in range(3)], g)
                for c in range(3):
                    n_buf[c, n, :, lanes] = a[c].astype(bf16)
            return carry

        lax.fori_loop(0, 8, block, 0)
        for copy in stores(ch, n_buf, nf_hbm, sem):
            copy.start()
    for ch in range(CHUNKS):
        for copy in stores(ch, n_buf, nf_hbm, sem):
            copy.wait()


def advance(grad, f_flat, base):
    n = f_flat.shape[1]
    vmem = pl.BlockSpec(memory_space=pltpu.VMEM)
    return pl.pallas_call(
        advance_kernel,
        out_shape=jax.ShapeDtypeStruct((3, n, 2, PLANES, 1024), bf16),
        in_specs=[vmem] * 3,
        out_specs=pl.BlockSpec(memory_space=pl.ANY),
        scratch_shapes=[pltpu.VMEM((3, n, 8, 1024), bf16), pltpu.SemaphoreType.DMA((CHUNKS, 6))],
        compiler_params=pltpu.CompilerParams(vmem_limit_bytes=16 << 20),
        cost_estimate=pl.CostEstimate(flops=6_000_000, bytes_accessed=6_000_000, transcendentals=0),
    )(grad, f_flat, base)


def body(velocity, pressure, fields, brownian):
    total = lax.axis_size("mesh") * PLANES

    def exchange(x, pairs):
        return lax.ppermute(x, AXES, pairs + [(b, a) for a, b in pairs])

    own = velocity.reshape(3, 8, 128)
    edge = exchange(own, [(i, i + 1) for i in range(PLANES - 1, total - 1, PLANES)])
    f_flat, base, local = relax(own, pressure.reshape(1, 8, 128), fields, brownian)
    near = lax.all_gather(jnp.stack([own, edge]), "field", axis=0)
    kept, outer, inner, grad = share(near, local, f_flat, base)

    neighbours = [(i, i + PLANES) for i in range(total - PLANES)]
    inner = exchange(inner, [p for p in neighbours if p[0] // PLANES % 2 == 0])
    outer = exchange(outer, [p for p in neighbours if p[0] // PLANES % 2 == 1])
    kept, new_fields = lax.optimization_barrier((kept, advance(grad, f_flat, base)))
    parts = lax.all_to_all(kept + (outer + inner), "field", 0, 0, tiled=True)
    result = (parts[0] + parts[1]) + (parts[2] + parts[3])
    return new_fields.reshape(fields.shape), result.reshape(velocity.shape)


def solution(mesh):
    placed = (
        P(None, ("mesh", "field"), None),
        P(("mesh", "field"), None),
        P(None, "field", "mesh", None),
        P(None, "field", "mesh", None),
    )
    return jax.shard_map(
        body,
        mesh=mesh,
        in_specs=placed,
        out_specs=(P(None, "field", "mesh", None), P(None, ("mesh", "field"), None)),
        check_vma=False,
    )
```

```python
import functools

import jax
import jax.numpy as jnp
from jax import lax
from jax.experimental import pallas as pl
from jax.experimental.pallas import tpu as pltpu
from jax.sharding import PartitionSpec as P

f32 = jnp.float32
bf16 = jnp.bfloat16

NF = 256
TIME_STEP = 0.02
AXIAL = 400.0
TRANSVERSE = 40.0
MAX_STRETCH = 50.0
VISCOSITY = 40.0
WEISSENBERG = 0.5
NOISE = (0.02 / 0.5) ** 0.5
DIAGONAL = 1.0 / 0.02 + 2.0 * 400.0 + 4.0 * 40.0
SWEEPS = 4
INDEX = ((0, 1, 2), (1, 3, 4), (2, 4, 5))
DIAGONAL_PAIRS = (0, 3, 5)

PLANES = 4
CHUNKS = 4
AXES = ("mesh", "field")


def lane_masks():
    lane = lax.broadcasted_iota(jnp.int32, (8, 128), 1)
    row = lax.broadcasted_iota(jnp.int32, (8, 128), 0)
    return dict(
        z_hi=(lane % 32) < 31,
        z_lo=(lane % 32) > 0,
        lane_hi=lane < 96,
        lane_lo=lane >= 32,
        row_hi=row < 7,
        row_lo=row > 0,
        channel=(row >= 2) & (row < 6),
    )


def shift_z(v, masks):
    plus = jnp.where(masks["z_hi"], pltpu.roll(v, 127, 1), 0.0)
    minus = jnp.where(masks["z_lo"], pltpu.roll(v, 1, 1), 0.0)
    return plus, minus


def shift_y(v, masks):
    ahead = pltpu.roll(v, 96, 1)
    behind = pltpu.roll(v, 32, 1)
    next_row = jnp.where(masks["row_hi"], pltpu.roll(ahead, 7, 0), 0.0)
    last_row = jnp.where(masks["row_lo"], pltpu.roll(behind, 1, 0), 0.0)
    return jnp.where(masks["lane_hi"], ahead, next_row), jnp.where(masks["lane_lo"], behind, last_row)


def slope_y(v, masks):
    plus, minus = shift_y(v, masks)
    return (plus - minus) * 0.5


def slope_z(v, masks):
    plus, minus = shift_z(v, masks)
    return (plus - minus) * 0.5


def around(v, masks):
    y_plus, y_minus = shift_y(v, masks)
    z_plus, z_minus = shift_z(v, masks)
    return (y_plus + y_minus) + (z_plus + z_minus)


def chunk(ch, pairs):
    per = pairs // CHUNKS
    return pl.ds(ch * per, per)


def loads(ch, sources, buffers, sem):
    some = chunk(ch, buffers[0].shape[1])
    return [
        pltpu.make_async_copy(src.at[c, some, h], buf.at[c, some, pl.ds(4 * h, 4), :], sem.at[ch, 6 * w + 2 * c + h])
        for w, (src, buf) in enumerate(zip(sources, buffers))
        for c in range(3)
        for h in range(2)
    ]


def stores(ch, buf, dst, sem):
    some = chunk(ch, buf.shape[1])
    return [
        pltpu.make_async_copy(buf.at[c, some, pl.ds(4 * h, 4), :], dst.at[c, some, h], sem.at[ch, 2 * c + h])
        for c in range(3)
        for h in range(2)
    ]


def relax_kernel(velocity_hbm, pressure_hbm, f_hbm, b_hbm, f_ref, base_ref, local_ref, b_buf, sem, local_sem):
    pairs = b_buf.shape[1]
    per = pairs // CHUNKS
    for ch in range(CHUNKS):
        for copy in loads(ch, (f_hbm, b_hbm), (f_ref, b_buf), sem):
            copy.start()
    own = (
        pltpu.make_async_copy(velocity_hbm, local_ref.at[pl.ds(0, 3)], local_sem.at[0]),
        pltpu.make_async_copy(pressure_hbm, local_ref.at[pl.ds(3, 1)], local_sem.at[1]),
    )
    for copy in own:
        copy.start()
    for ch in range(CHUNKS):
        for copy in loads(ch, (f_hbm, b_hbm), (f_ref, b_buf), sem):
            copy.wait()

        def block(j, carry):
            lanes = pl.ds(pl.multiple_of(128 * j, 128), 128)
            for u in range(per):
                n = ch * per + u
                f = [f_ref[c, n, :, lanes].astype(f32) for c in range(3)]
                length_sq = f[0] * f[0] + f[1] * f[1] + f[2] * f[2]
                pull = TIME_STEP * MAX_STRETCH / (2.0 * WEISSENBERG) * pltpu.reciprocal(MAX_STRETCH - length_sq)
                kept = 1.0 - pull
                for c in range(3):
                    base_ref[c, n, :, lanes] = kept * f[c] + NOISE * b_buf[c, n, :, lanes].astype(f32)
            return carry

        lax.fori_loop(0, 8, block, 0)
    for copy in own:
        copy.wait()


def in_hbm(x):
    return pltpu.with_memory_space_constraint(x, pltpu.HBM)


def relax(velocity, pressure, fields, brownian):
    n = fields.shape[1] // 2
    split = (3, n, 2, PLANES, 1024)
    flat = (3, n, 8, 1024)
    vmem = pl.BlockSpec(memory_space=pltpu.VMEM)
    hbm = pl.BlockSpec(memory_space=pl.ANY)
    return pl.pallas_call(
        relax_kernel,
        out_shape=(
            jax.ShapeDtypeStruct(flat, bf16),
            jax.ShapeDtypeStruct(flat, f32),
            jax.ShapeDtypeStruct((4, 8, 128), f32),
        ),
        in_specs=[hbm] * 4,
        out_specs=[vmem, vmem, vmem],
        scratch_shapes=[
            pltpu.VMEM(flat, bf16),
            pltpu.SemaphoreType.DMA((CHUNKS, 12)),
            pltpu.SemaphoreType.DMA((2,)),
        ],
        compiler_params=pltpu.CompilerParams(vmem_limit_bytes=24 << 20),
        cost_estimate=pl.CostEstimate(flops=10_000_000, bytes_accessed=8_000_000, transcendentals=0),
    )(*(in_hbm(x) for x in (velocity, pressure, fields.reshape(split), brownian.reshape(split))))


def stretch(f, base, g):
    return [base[o] + (g[3 * o] * f[0] + g[3 * o + 1] * f[1] + g[3 * o + 2] * f[2]) for o in range(3)]


def share_kernel(
    slabs, near_ref, local_ref, f_ref, base_ref, nf_hbm, own_ref, outer_ref, inner_ref, n_buf, grad, sums, sem
):
    pairs = f_ref.shape[1]
    per = pairs // CHUNKS
    slab = lax.axis_index("mesh")
    mine = lax.axis_index("field")
    masks = lane_masks()

    planes = [(0, 1), (0, 0), (1, 0), (2, 0), (3, 0), (3, 1)]
    for q in range(PLANES):
        for a in range(3):
            before, centre, after = (near_ref[d, e, a] for d, e in planes[q : q + 3])
            slopes = ((after - before) * 0.5, slope_y(centre, masks), slope_z(centre, masks))
            for c in range(3):
                value = slopes[c] * TIME_STEP
                grad[3 * a + c, pl.ds(q, 8, stride=8), :] = value
                grad[3 * a + c, pl.ds(q + 4, 8, stride=8), :] = value

    for ch in range(CHUNKS):

        def block(j, carry):
            rows = pl.ds(pl.multiple_of(8 * j, 8), 8)
            lanes = pl.ds(pl.multiple_of(128 * j, 128), 128)
            g = [grad[k, rows, :] for k in range(9)]
            if ch:
                acc = [sums[k, rows, :] for k in range(6)]
            else:
                acc = [jnp.zeros((8, 128), f32) for _ in range(6)]
            for u in range(per):
                n = ch * per + u
                f = [f_ref[c, n, :, lanes].astype(f32) for c in range(3)]
                a = stretch(f, [base_ref[o, n, :, lanes] for o in range(3)], g)
                for c in range(3):
                    n_buf[c, n, :, lanes] = a[c].astype(bf16)
                s = [x * x for x in a]
                r = pltpu.reciprocal(MAX_STRETCH - (s[0] + s[1] + s[2]))
                p0 = r * a[0]
                p1 = r * a[1]
                products = (r * s[0], p0 * a[1], p0 * a[2], r * s[1], p1 * a[2], r * s[2])
                acc = [x + y for x, y in zip(acc, products)]
            for k in range(6):
                sums[k, rows, :] = acc[k]
            return carry

        lax.fori_loop(0, 8, block, 0)
        for copy in stores(ch, n_buf, nf_hbm, sem):
            copy.start()

    scale = VISCOSITY / WEISSENBERG / NF * MAX_STRETCH
    stress = []
    for k in range(6):
        rows = []
        for q in range(PLANES):
            total = sums[k, pl.ds(q, 8, stride=8), :] + sums[k, pl.ds(q + 4, 8, stride=8), :]
            total = total * scale
            if k in DIAGONAL_PAIRS:
                total = total - VISCOSITY / WEISSENBERG / 4
            rows.append(total)
        stress.append(rows)

    own = [mine == q for q in range(PLANES)]
    zero = jnp.zeros((8, 128), f32)
    pressure = [jnp.where(own[q], local_ref[3], 0.0) for q in range(PLANES)]
    start = [[jnp.where(own[q], local_ref[a], 0.0) for q in range(PLANES)] for a in range(3)]

    def at(values, q):
        return values[q] if 0 <= q < PLANES else None

    def add(x, y):
        return y if x is None else x if y is None else x + y

    def halfway(values, q):
        plus, minus = at(values, q + 1), at(values, q - 1)
        if plus is None:
            return None if minus is None else minus * -0.5
        return plus * 0.5 if minus is None else (plus - minus) * 0.5

    first = -(SWEEPS)
    count = PLANES + 2 * SWEEPS
    fluid = []
    for q in range(first, first + count):
        plane = slab * PLANES + q
        inside = (plane >= 0) & (plane < slabs * PLANES)
        wide = plane < slabs * PLANES // 2
        value = jnp.where(masks["channel"] | wide, 1.0 / DIAGONAL, 0.0)
        fluid.append(jnp.where(inside, value, 0.0))

    for a in range(3):
        source = {}
        for q in range(-1, PLANES + 1):
            total = halfway(stress[INDEX[a][0]], q)
            if a == 0:
                total = total - halfway(pressure, q) if total is not None else None
            if 0 <= q < PLANES:
                inner = slope_y(stress[INDEX[a][1]][q], masks) + slope_z(stress[INDEX[a][2]][q], masks)
                if a == 1:
                    inner = inner - slope_y(pressure[q], masks)
                if a == 2:
                    inner = inner - slope_z(pressure[q], masks)
                total = total + inner + start[a][q] * (1.0 / TIME_STEP)
            source[q] = total
        current = {q: start[a][q] for q in range(PLANES)}
        for sweep in range(SWEEPS):
            later = {}
            for q in range(-1 - sweep, PLANES + 1 + sweep):
                total = source.get(q)
                along = add(current.get(q - 1), current.get(q + 1))
                if along is not None:
                    total = add(total, AXIAL * along)
                if q in current:
                    total = add(total, TRANSVERSE * around(current[q], masks))
                later[q] = total * fluid[q - first]
            current = later
        odd = slab % 2 == 1
        for q in range(PLANES):
            before, after = current[q - PLANES], current[q + PLANES]
            own_ref[q, a] = current[q]
            outer_ref[q, a] = jnp.where(odd, after, before)
            inner_ref[q, a] = jnp.where(odd, before, after)

    for ch in range(CHUNKS):
        for copy in stores(ch, n_buf, nf_hbm, sem):
            copy.wait()


def share(near, local, f_flat, base):
    n = f_flat.shape[1]
    slabs = lax.axis_size("mesh")
    vmem = pl.BlockSpec(memory_space=pltpu.VMEM)
    part = jax.ShapeDtypeStruct((PLANES, 3, 8, 128), f32)
    return pl.pallas_call(
        functools.partial(share_kernel, slabs),
        out_shape=(jax.ShapeDtypeStruct((3, n, 2, PLANES, 1024), bf16), part, part, part),
        in_specs=[vmem] * 4,
        out_specs=[pl.BlockSpec(memory_space=pl.ANY), vmem, vmem, vmem],
        scratch_shapes=[
            pltpu.VMEM((3, n, 8, 1024), bf16),
            pltpu.VMEM((9, 64, 128), f32),
            pltpu.VMEM((6, 64, 128), f32),
            pltpu.SemaphoreType.DMA((CHUNKS, 6)),
        ],
        compiler_params=pltpu.CompilerParams(vmem_limit_bytes=16 << 20),
        cost_estimate=pl.CostEstimate(flops=13_000_000, bytes_accessed=7_000_000, transcendentals=0),
    )(near, local, f_flat, base)


def body(velocity, pressure, fields, brownian):
    total = lax.axis_size("mesh") * PLANES

    def exchange(x, pairs):
        return lax.ppermute(x, AXES, pairs + [(b, a) for a, b in pairs])

    own = velocity.reshape(3, 8, 128)
    edge = exchange(own, [(i, i + 1) for i in range(PLANES - 1, total - 1, PLANES)])
    f_flat, base, local = relax(own, pressure.reshape(1, 8, 128), fields, brownian)
    near = lax.all_gather(jnp.stack([own, edge]), "field", axis=0)
    new_fields, kept, outer, inner = share(near, local, f_flat, base)

    outer = exchange(outer, [(i, i + PLANES) for i in range(total - PLANES) if i // PLANES % 2 == 1])
    couples = [[i, i + PLANES] for i in range(total) if i // PLANES % 2 == 0]
    both = lax.all_gather(inner, AXES, axis=0, axis_index_groups=couples)
    inner = jnp.where(lax.axis_index("mesh") % 2 == 1, both[0], both[1])
    parts = lax.all_to_all(kept + (outer + inner), "field", 0, 0, tiled=True)
    result = (parts[0] + parts[1]) + (parts[2] + parts[3])
    return new_fields.reshape(fields.shape), result.reshape(velocity.shape)


def solution(mesh):
    placed = (
        P(None, ("mesh", "field"), None),
        P(("mesh", "field"), None),
        P(None, "field", "mesh", None),
        P(None, "field", "mesh", None),
    )
    return jax.shard_map(
        body,
        mesh=mesh,
        in_specs=placed,
        out_specs=(P(None, "field", "mesh", None), P(None, ("mesh", "field"), None)),
        check_vma=False,
    )
```

```python
import functools

import jax
import jax.numpy as jnp
from jax import lax
from jax.experimental import pallas as pl
from jax.experimental.pallas import tpu as pltpu
from jax.sharding import PartitionSpec as P

f32 = jnp.float32
bf16 = jnp.bfloat16

NF = 256
TIME_STEP = 0.02
AXIAL = 400.0
TRANSVERSE = 40.0
MAX_STRETCH = 50.0
VISCOSITY = 40.0
WEISSENBERG = 0.5
NOISE = (0.02 / 0.5) ** 0.5
DIAGONAL = 1.0 / 0.02 + 2.0 * 400.0 + 4.0 * 40.0
SWEEPS = 4
INDEX = ((0, 1, 2), (1, 3, 4), (2, 4, 5))
DIAGONAL_PAIRS = (0, 3, 5)

PLANES = 4
BLOCKS = 8
UNROLL = 16
AXES = ("mesh", "field")


def lane_masks():
    lane = lax.broadcasted_iota(jnp.int32, (8, 128), 1)
    row = lax.broadcasted_iota(jnp.int32, (8, 128), 0)
    return dict(
        z_hi=(lane % 32) < 31,
        z_lo=(lane % 32) > 0,
        lane_hi=lane < 96,
        lane_lo=lane >= 32,
        row_hi=row < 7,
        row_lo=row > 0,
        channel=(row >= 2) & (row < 6),
    )


def shift_z(v, masks):
    plus = jnp.where(masks["z_hi"], pltpu.roll(v, 127, 1), 0.0)
    minus = jnp.where(masks["z_lo"], pltpu.roll(v, 1, 1), 0.0)
    return plus, minus


def shift_y(v, masks):
    ahead = pltpu.roll(v, 96, 1)
    behind = pltpu.roll(v, 32, 1)
    next_row = jnp.where(masks["row_hi"], pltpu.roll(ahead, 7, 0), 0.0)
    last_row = jnp.where(masks["row_lo"], pltpu.roll(behind, 1, 0), 0.0)
    return jnp.where(masks["lane_hi"], ahead, next_row), jnp.where(masks["lane_lo"], behind, last_row)


def slope_y(v, masks):
    plus, minus = shift_y(v, masks)
    return (plus - minus) * 0.5


def slope_z(v, masks):
    plus, minus = shift_z(v, masks)
    return (plus - minus) * 0.5


def around(v, masks):
    y_plus, y_minus = shift_y(v, masks)
    z_plus, z_minus = shift_z(v, masks)
    return (y_plus + y_minus) + (z_plus + z_minus)


def lanes_of(j):
    return pl.ds(pl.multiple_of(128 * j, 128), 128)


def loads(j, sources, buffers, sem):
    lanes = lanes_of(j)
    return [
        pltpu.make_async_copy(src.at[:, :, h, :, lanes], buf.at[:, :, pl.ds(4 * h, 4), lanes], sem.at[j, 2 * w + h])
        for w, (src, buf) in enumerate(zip(sources, buffers))
        for h in range(2)
    ]


def stores(j, buf, dst, sem):
    lanes = lanes_of(j)
    return [
        pltpu.make_async_copy(buf.at[:, :, pl.ds(4 * h, 4), lanes], dst.at[:, :, h, :, lanes], sem.at[j, h])
        for h in range(2)
    ]


def relax_kernel(velocity_hbm, pressure_hbm, f_hbm, b_hbm, f_ref, base_ref, local_ref, b_buf, sem, local_sem):
    pairs = b_buf.shape[1]

    def begin(j, carry):
        for copy in loads(j, (f_hbm, b_hbm), (f_ref, b_buf), sem):
            copy.start()
        return carry

    lax.fori_loop(0, BLOCKS, begin, 0)
    own = (
        pltpu.make_async_copy(velocity_hbm, local_ref.at[pl.ds(0, 3)], local_sem.at[0]),
        pltpu.make_async_copy(pressure_hbm, local_ref.at[pl.ds(3, 1)], local_sem.at[1]),
    )
    for copy in own:
        copy.start()

    def block(j, carry):
        lanes = lanes_of(j)
        for copy in loads(j, (f_hbm, b_hbm), (f_ref, b_buf), sem):
            copy.wait()

        def some(i, inner):
            for u in range(UNROLL):
                n = i * UNROLL + u
                f = [f_ref[c, n, :, lanes].astype(f32) for c in range(3)]
                length_sq = f[0] * f[0] + f[1] * f[1] + f[2] * f[2]
                pull = TIME_STEP * MAX_STRETCH / (2.0 * WEISSENBERG) * pltpu.reciprocal(MAX_STRETCH - length_sq)
                kept = 1.0 - pull
                for c in range(3):
                    base_ref[c, n, :, lanes] = kept * f[c] + NOISE * b_buf[c, n, :, lanes].astype(f32)
            return inner

        return lax.fori_loop(0, pairs // UNROLL, some, carry)

    lax.fori_loop(0, BLOCKS, block, 0)
    for copy in own:
        copy.wait()


def in_hbm(x):
    return pltpu.with_memory_space_constraint(x, pltpu.HBM)


def relax(velocity, pressure, fields, brownian):
    n = fields.shape[1] // 2
    split = (3, n, 2, PLANES, 1024)
    flat = (3, n, 8, 1024)
    vmem = pl.BlockSpec(memory_space=pltpu.VMEM)
    hbm = pl.BlockSpec(memory_space=pl.ANY)
    return pl.pallas_call(
        relax_kernel,
        out_shape=(
            jax.ShapeDtypeStruct(flat, bf16),
            jax.ShapeDtypeStruct(flat, f32),
            jax.ShapeDtypeStruct((4, 8, 128), f32),
        ),
        in_specs=[hbm] * 4,
        out_specs=[vmem, vmem, vmem],
        scratch_shapes=[
            pltpu.VMEM(flat, bf16),
            pltpu.SemaphoreType.DMA((BLOCKS, 4)),
            pltpu.SemaphoreType.DMA((2,)),
        ],
        compiler_params=pltpu.CompilerParams(vmem_limit_bytes=24 << 20),
        cost_estimate=pl.CostEstimate(flops=10_000_000, bytes_accessed=8_000_000, transcendentals=0),
    )(*(in_hbm(x) for x in (velocity, pressure, fields.reshape(split), brownian.reshape(split))))


def stretch(f, base, g):
    return [base[o] + (g[3 * o] * f[0] + g[3 * o + 1] * f[1] + g[3 * o + 2] * f[2]) for o in range(3)]


def share_kernel(
    slabs, near_ref, local_ref, f_ref, base_ref, nf_hbm, own_ref, outer_ref, inner_ref, n_buf, grad, sums, sem
):
    pairs = f_ref.shape[1]
    slab = lax.axis_index("mesh")
    mine = lax.axis_index("field")
    masks = lane_masks()

    planes = [(0, 1), (0, 0), (1, 0), (2, 0), (3, 0), (3, 1)]
    for q in range(PLANES):
        for a in range(3):
            before, centre, after = (near_ref[d, e, a] for d, e in planes[q : q + 3])
            slopes = ((after - before) * 0.5, slope_y(centre, masks), slope_z(centre, masks))
            for c in range(3):
                value = slopes[c] * TIME_STEP
                grad[3 * a + c, pl.ds(q, 8, stride=8), :] = value
                grad[3 * a + c, pl.ds(q + 4, 8, stride=8), :] = value

    def block(j, carry):
        rows = pl.ds(pl.multiple_of(8 * j, 8), 8)
        lanes = lanes_of(j)
        g = [grad[k, rows, :] for k in range(9)]

        def some(i, acc):
            for u in range(UNROLL):
                n = i * UNROLL + u
                f = [f_ref[c, n, :, lanes].astype(f32) for c in range(3)]
                a = stretch(f, [base_ref[o, n, :, lanes] for o in range(3)], g)
                for c in range(3):
                    n_buf[c, n, :, lanes] = a[c].astype(bf16)
                s = [x * x for x in a]
                r = pltpu.reciprocal(MAX_STRETCH - (s[0] + s[1] + s[2]))
                p0 = r * a[0]
                p1 = r * a[1]
                products = (r * s[0], p0 * a[1], p0 * a[2], r * s[1], p1 * a[2], r * s[2])
                acc = tuple(x + y for x, y in zip(acc, products))
            return acc

        acc = lax.fori_loop(0, pairs // UNROLL, some, tuple(jnp.zeros((8, 128), f32) for _ in range(6)))
        for k in range(6):
            sums[k, rows, :] = acc[k]
        for copy in stores(j, n_buf, nf_hbm, sem):
            copy.start()
        return carry

    lax.fori_loop(0, BLOCKS, block, 0)

    scale = VISCOSITY / WEISSENBERG / NF * MAX_STRETCH
    stress = []
    for k in range(6):
        rows = []
        for q in range(PLANES):
            total = sums[k, pl.ds(q, 8, stride=8), :] + sums[k, pl.ds(q + 4, 8, stride=8), :]
            total = total * scale
            if k in DIAGONAL_PAIRS:
                total = total - VISCOSITY / WEISSENBERG / 4
            rows.append(total)
        stress.append(rows)

    own = [mine == q for q in range(PLANES)]
    zero = jnp.zeros((8, 128), f32)
    pressure = [jnp.where(own[q], local_ref[3], 0.0) for q in range(PLANES)]
    start = [[jnp.where(own[q], local_ref[a], 0.0) for q in range(PLANES)] for a in range(3)]

    def at(values, q):
        return values[q] if 0 <= q < PLANES else None

    def add(x, y):
        return y if x is None else x if y is None else x + y

    def halfway(values, q):
        plus, minus = at(values, q + 1), at(values, q - 1)
        if plus is None:
            return None if minus is None else minus * -0.5
        return plus * 0.5 if minus is None else (plus - minus) * 0.5

    first = -(SWEEPS)
    count = PLANES + 2 * SWEEPS
    fluid = []
    for q in range(first, first + count):
        plane = slab * PLANES + q
        inside = (plane >= 0) & (plane < slabs * PLANES)
        wide = plane < slabs * PLANES // 2
        value = jnp.where(masks["channel"] | wide, 1.0 / DIAGONAL, 0.0)
        fluid.append(jnp.where(inside, value, 0.0))

    for a in range(3):
        source = {}
        for q in range(-1, PLANES + 1):
            total = halfway(stress[INDEX[a][0]], q)
            if a == 0:
                total = total - halfway(pressure, q) if total is not None else None
            if 0 <= q < PLANES:
                inner = slope_y(stress[INDEX[a][1]][q], masks) + slope_z(stress[INDEX[a][2]][q], masks)
                if a == 1:
                    inner = inner - slope_y(pressure[q], masks)
                if a == 2:
                    inner = inner - slope_z(pressure[q], masks)
                total = total + inner + start[a][q] * (1.0 / TIME_STEP)
            source[q] = total
        current = {q: start[a][q] for q in range(PLANES)}
        for sweep in range(SWEEPS):
            later = {}
            for q in range(-1 - sweep, PLANES + 1 + sweep):
                total = source.get(q)
                along = add(current.get(q - 1), current.get(q + 1))
                if along is not None:
                    total = add(total, AXIAL * along)
                if q in current:
                    total = add(total, TRANSVERSE * around(current[q], masks))
                later[q] = total * fluid[q - first]
            current = later
        odd = slab % 2 == 1
        for q in range(PLANES):
            before, after = current[q - PLANES], current[q + PLANES]
            own_ref[q, a] = current[q]
            outer_ref[q, a] = jnp.where(odd, after, before)
            inner_ref[q, a] = jnp.where(odd, before, after)

    def end(j, carry):
        for copy in stores(j, n_buf, nf_hbm, sem):
            copy.wait()
        return carry

    lax.fori_loop(0, BLOCKS, end, 0)


def share(near, local, f_flat, base):
    n = f_flat.shape[1]
    slabs = lax.axis_size("mesh")
    vmem = pl.BlockSpec(memory_space=pltpu.VMEM)
    part = jax.ShapeDtypeStruct((PLANES, 3, 8, 128), f32)
    return pl.pallas_call(
        functools.partial(share_kernel, slabs),
        out_shape=(jax.ShapeDtypeStruct((3, n, 2, PLANES, 1024), bf16), part, part, part),
        in_specs=[vmem] * 4,
        out_specs=[pl.BlockSpec(memory_space=pl.ANY), vmem, vmem, vmem],
        scratch_shapes=[
            pltpu.VMEM((3, n, 8, 1024), bf16),
            pltpu.VMEM((9, 64, 128), f32),
            pltpu.VMEM((6, 64, 128), f32),
            pltpu.SemaphoreType.DMA((BLOCKS, 2)),
        ],
        compiler_params=pltpu.CompilerParams(vmem_limit_bytes=16 << 20),
        cost_estimate=pl.CostEstimate(flops=13_000_000, bytes_accessed=7_000_000, transcendentals=0),
    )(near, local, f_flat, base)


def body(velocity, pressure, fields, brownian):
    total = lax.axis_size("mesh") * PLANES

    def exchange(x, pairs):
        return lax.ppermute(x, AXES, pairs + [(b, a) for a, b in pairs])

    own = velocity.reshape(3, 8, 128)
    edge = exchange(own, [(i, i + 1) for i in range(PLANES - 1, total - 1, PLANES)])
    f_flat, base, local = relax(own, pressure.reshape(1, 8, 128), fields, brownian)
    near = lax.all_gather(jnp.stack([own, edge]), "field", axis=0)
    new_fields, kept, outer, inner = share(near, local, f_flat, base)

    outer = exchange(outer, [(i, i + PLANES) for i in range(total - PLANES) if i // PLANES % 2 == 1])
    couples = [[i, i + PLANES] for i in range(total) if i // PLANES % 2 == 0]
    both = lax.all_gather(inner, AXES, axis=0, axis_index_groups=couples)
    inner = jnp.where(lax.axis_index("mesh") % 2 == 1, both[0], both[1])
    parts = lax.all_to_all(kept + (outer + inner), "field", 0, 0, tiled=True)
    result = (parts[0] + parts[1]) + (parts[2] + parts[3])
    return new_fields.reshape(fields.shape), result.reshape(velocity.shape)


def solution(mesh):
    placed = (
        P(None, ("mesh", "field"), None),
        P(("mesh", "field"), None),
        P(None, "field", "mesh", None),
        P(None, "field", "mesh", None),
    )
    return jax.shard_map(
        body,
        mesh=mesh,
        in_specs=placed,
        out_specs=(P(None, "field", "mesh", None), P(None, ("mesh", "field"), None)),
        check_vma=False,
    )
```

```python
import functools

import jax
import jax.numpy as jnp
from jax import lax
from jax.experimental import pallas as pl
from jax.experimental.pallas import tpu as pltpu
from jax.sharding import PartitionSpec as P

f32 = jnp.float32
bf16 = jnp.bfloat16

NF = 256
TIME_STEP = 0.02
AXIAL = 400.0
TRANSVERSE = 40.0
MAX_STRETCH = 50.0
VISCOSITY = 40.0
WEISSENBERG = 0.5
NOISE = (0.02 / 0.5) ** 0.5
DIAGONAL = 1.0 / 0.02 + 2.0 * 400.0 + 4.0 * 40.0
SWEEPS = 4
INDEX = ((0, 1, 2), (1, 3, 4), (2, 4, 5))
DIAGONAL_PAIRS = (0, 3, 5)

PLANES = 4
BLOCKS = 8
UNROLL = 16
AXES = ("mesh", "field")


def lane_masks():
    lane = lax.broadcasted_iota(jnp.int32, (8, 128), 1)
    row = lax.broadcasted_iota(jnp.int32, (8, 128), 0)
    return dict(
        z_hi=(lane % 32) < 31,
        z_lo=(lane % 32) > 0,
        lane_hi=lane < 96,
        lane_lo=lane >= 32,
        row_hi=row < 7,
        row_lo=row > 0,
        channel=(row >= 2) & (row < 6),
    )


def shift_z(v, masks):
    plus = jnp.where(masks["z_hi"], pltpu.roll(v, 127, 1), 0.0)
    minus = jnp.where(masks["z_lo"], pltpu.roll(v, 1, 1), 0.0)
    return plus, minus


def shift_y(v, masks):
    ahead = pltpu.roll(v, 96, 1)
    behind = pltpu.roll(v, 32, 1)
    next_row = jnp.where(masks["row_hi"], pltpu.roll(ahead, 7, 0), 0.0)
    last_row = jnp.where(masks["row_lo"], pltpu.roll(behind, 1, 0), 0.0)
    return jnp.where(masks["lane_hi"], ahead, next_row), jnp.where(masks["lane_lo"], behind, last_row)


def slope_y(v, masks):
    plus, minus = shift_y(v, masks)
    return (plus - minus) * 0.5


def slope_z(v, masks):
    plus, minus = shift_z(v, masks)
    return (plus - minus) * 0.5


def around(v, masks):
    y_plus, y_minus = shift_y(v, masks)
    z_plus, z_minus = shift_z(v, masks)
    return (y_plus + y_minus) + (z_plus + z_minus)


def lanes_of(j):
    return pl.ds(pl.multiple_of(128 * j, 128), 128)


def loads(j, sources, buffers, sem):
    lanes = lanes_of(j)
    return [
        pltpu.make_async_copy(src.at[:, :, h, :, lanes], buf.at[:, :, pl.ds(4 * h, 4), lanes], sem.at[j, 2 * w + h])
        for w, (src, buf) in enumerate(zip(sources, buffers))
        for h in range(2)
    ]


def stores(j, buf, dst, sem):
    lanes = lanes_of(j)
    return [
        pltpu.make_async_copy(buf.at[:, :, pl.ds(4 * h, 4), lanes], dst.at[:, :, h, :, lanes], sem.at[j, h])
        for h in range(2)
    ]


def relax_kernel(velocity_hbm, pressure_hbm, f_hbm, b_hbm, f_ref, base_ref, local_ref, f_buf, b_buf, sem, local_sem):
    pairs = b_buf.shape[1]

    def begin(j, carry):
        for copy in loads(j, (f_hbm, b_hbm), (f_buf, b_buf), sem):
            copy.start()
        return carry

    lax.fori_loop(0, BLOCKS, begin, 0)
    own = (
        pltpu.make_async_copy(velocity_hbm, local_ref.at[pl.ds(0, 3)], local_sem.at[0]),
        pltpu.make_async_copy(pressure_hbm, local_ref.at[pl.ds(3, 1)], local_sem.at[1]),
    )
    for copy in own:
        copy.start()

    def block(j, carry):
        lanes = lanes_of(j)
        for copy in loads(j, (f_hbm, b_hbm), (f_buf, b_buf), sem):
            copy.wait()

        def some(i, inner):
            for u in range(UNROLL):
                n = i * UNROLL + u
                f = [f_buf[c, n, :, lanes].astype(f32) for c in range(3)]
                length_sq = f[0] * f[0] + f[1] * f[1] + f[2] * f[2]
                pull = TIME_STEP * MAX_STRETCH / (2.0 * WEISSENBERG) * pltpu.reciprocal(MAX_STRETCH - length_sq)
                kept = 1.0 - pull
                for c in range(3):
                    f_ref[c, n, :, lanes] = f[c]
                    base_ref[c, n, :, lanes] = kept * f[c] + NOISE * b_buf[c, n, :, lanes].astype(f32)
            return inner

        return lax.fori_loop(0, pairs // UNROLL, some, carry)

    lax.fori_loop(0, BLOCKS, block, 0)
    for copy in own:
        copy.wait()


def in_hbm(x):
    return pltpu.with_memory_space_constraint(x, pltpu.HBM)


def relax(velocity, pressure, fields, brownian):
    n = fields.shape[1] // 2
    split = (3, n, 2, PLANES, 1024)
    flat = (3, n, 8, 1024)
    vmem = pl.BlockSpec(memory_space=pltpu.VMEM)
    hbm = pl.BlockSpec(memory_space=pl.ANY)
    return pl.pallas_call(
        relax_kernel,
        out_shape=(
            jax.ShapeDtypeStruct(flat, f32),
            jax.ShapeDtypeStruct(flat, f32),
            jax.ShapeDtypeStruct((4, 8, 128), f32),
        ),
        in_specs=[hbm] * 4,
        out_specs=[vmem, vmem, vmem],
        scratch_shapes=[
            pltpu.VMEM(flat, bf16),
            pltpu.VMEM(flat, bf16),
            pltpu.SemaphoreType.DMA((BLOCKS, 4)),
            pltpu.SemaphoreType.DMA((2,)),
        ],
        compiler_params=pltpu.CompilerParams(vmem_limit_bytes=24 << 20),
        cost_estimate=pl.CostEstimate(flops=10_000_000, bytes_accessed=8_000_000, transcendentals=0),
    )(*(in_hbm(x) for x in (velocity, pressure, fields.reshape(split), brownian.reshape(split))))


def stretch(f, base, g):
    return [base[o] + (g[3 * o] * f[0] + g[3 * o + 1] * f[1] + g[3 * o + 2] * f[2]) for o in range(3)]


def share_kernel(
    slabs, near_ref, local_ref, f_ref, base_ref, nf_hbm, own_ref, outer_ref, inner_ref, n_buf, grad, sums, sem
):
    pairs = f_ref.shape[1]
    slab = lax.axis_index("mesh")
    mine = lax.axis_index("field")
    masks = lane_masks()

    planes = [(0, 1), (0, 0), (1, 0), (2, 0), (3, 0), (3, 1)]
    for q in range(PLANES):
        for a in range(3):
            before, centre, after = (near_ref[d, e, a] for d, e in planes[q : q + 3])
            slopes = ((after - before) * 0.5, slope_y(centre, masks), slope_z(centre, masks))
            for c in range(3):
                value = slopes[c] * TIME_STEP
                grad[3 * a + c, pl.ds(q, 8, stride=8), :] = value
                grad[3 * a + c, pl.ds(q + 4, 8, stride=8), :] = value

    def block(j, carry):
        rows = pl.ds(pl.multiple_of(8 * j, 8), 8)
        lanes = lanes_of(j)
        g = [grad[k, rows, :] for k in range(9)]

        def some(i, acc):
            for u in range(UNROLL):
                n = i * UNROLL + u
                f = [f_ref[c, n, :, lanes] for c in range(3)]
                a = stretch(f, [base_ref[o, n, :, lanes] for o in range(3)], g)
                for c in range(3):
                    n_buf[c, n, :, lanes] = a[c].astype(bf16)
                s = [x * x for x in a]
                r = pltpu.reciprocal(MAX_STRETCH - (s[0] + s[1] + s[2]))
                p0 = r * a[0]
                p1 = r * a[1]
                products = (r * s[0], p0 * a[1], p0 * a[2], r * s[1], p1 * a[2], r * s[2])
                acc = tuple(x + y for x, y in zip(acc, products))
            return acc

        acc = lax.fori_loop(0, pairs // UNROLL, some, tuple(jnp.zeros((8, 128), f32) for _ in range(6)))
        for k in range(6):
            sums[k, rows, :] = acc[k]
        for copy in stores(j, n_buf, nf_hbm, sem):
            copy.start()
        return carry

    lax.fori_loop(0, BLOCKS, block, 0)

    scale = VISCOSITY / WEISSENBERG / NF * MAX_STRETCH
    stress = []
    for k in range(6):
        rows = []
        for q in range(PLANES):
            total = sums[k, pl.ds(q, 8, stride=8), :] + sums[k, pl.ds(q + 4, 8, stride=8), :]
            total = total * scale
            if k in DIAGONAL_PAIRS:
                total = total - VISCOSITY / WEISSENBERG / 4
            rows.append(total)
        stress.append(rows)

    own = [mine == q for q in range(PLANES)]
    zero = jnp.zeros((8, 128), f32)
    pressure = [jnp.where(own[q], local_ref[3], 0.0) for q in range(PLANES)]
    start = [[jnp.where(own[q], local_ref[a], 0.0) for q in range(PLANES)] for a in range(3)]

    def at(values, q):
        return values[q] if 0 <= q < PLANES else None

    def add(x, y):
        return y if x is None else x if y is None else x + y

    def halfway(values, q):
        plus, minus = at(values, q + 1), at(values, q - 1)
        if plus is None:
            return None if minus is None else minus * -0.5
        return plus * 0.5 if minus is None else (plus - minus) * 0.5

    first = -(SWEEPS)
    count = PLANES + 2 * SWEEPS
    fluid = []
    for q in range(first, first + count):
        plane = slab * PLANES + q
        inside = (plane >= 0) & (plane < slabs * PLANES)
        wide = plane < slabs * PLANES // 2
        value = jnp.where(masks["channel"] | wide, 1.0 / DIAGONAL, 0.0)
        fluid.append(jnp.where(inside, value, 0.0))

    sources, currents = [], [{q: start[a][q] for q in range(PLANES)} for a in range(3)]
    for a in range(3):
        source = {}
        for q in range(-1, PLANES + 1):
            total = halfway(stress[INDEX[a][0]], q)
            if a == 0:
                total = total - halfway(pressure, q) if total is not None else None
            if 0 <= q < PLANES:
                inner = slope_y(stress[INDEX[a][1]][q], masks) + slope_z(stress[INDEX[a][2]][q], masks)
                if a == 1:
                    inner = inner - slope_y(pressure[q], masks)
                if a == 2:
                    inner = inner - slope_z(pressure[q], masks)
                total = total + inner + start[a][q] * (1.0 / TIME_STEP)
            source[q] = total
        sources.append(source)
    for sweep in range(SWEEPS):
        for a in range(3):
            current = currents[a]
            later = {}
            for q in range(-1 - sweep, PLANES + 1 + sweep):
                total = sources[a].get(q)
                along = add(current.get(q - 1), current.get(q + 1))
                if along is not None:
                    total = add(total, AXIAL * along)
                if q in current:
                    total = add(total, TRANSVERSE * around(current[q], masks))
                later[q] = total * fluid[q - first]
            currents[a] = later
    odd = slab % 2 == 1
    for a in range(3):
        for q in range(PLANES):
            before, after = currents[a][q - PLANES], currents[a][q + PLANES]
            own_ref[q, a] = currents[a][q]
            outer_ref[q, a] = jnp.where(odd, after, before)
            inner_ref[q, a] = jnp.where(odd, before, after)

    def end(j, carry):
        for copy in stores(j, n_buf, nf_hbm, sem):
            copy.wait()
        return carry

    lax.fori_loop(0, BLOCKS, end, 0)


def share(near, local, f_flat, base):
    n = f_flat.shape[1]
    slabs = lax.axis_size("mesh")
    vmem = pl.BlockSpec(memory_space=pltpu.VMEM)
    part = jax.ShapeDtypeStruct((PLANES, 3, 8, 128), f32)
    return pl.pallas_call(
        functools.partial(share_kernel, slabs),
        out_shape=(jax.ShapeDtypeStruct((3, n, 2, PLANES, 1024), bf16), part, part, part),
        in_specs=[vmem] * 4,
        out_specs=[pl.BlockSpec(memory_space=pl.ANY), vmem, vmem, vmem],
        scratch_shapes=[
            pltpu.VMEM((3, n, 8, 1024), bf16),
            pltpu.VMEM((9, 64, 128), f32),
            pltpu.VMEM((6, 64, 128), f32),
            pltpu.SemaphoreType.DMA((BLOCKS, 2)),
        ],
        compiler_params=pltpu.CompilerParams(vmem_limit_bytes=16 << 20),
        cost_estimate=pl.CostEstimate(flops=13_000_000, bytes_accessed=7_000_000, transcendentals=0),
    )(near, local, f_flat, base)


def body(velocity, pressure, fields, brownian):
    total = lax.axis_size("mesh") * PLANES

    def exchange(x, pairs):
        return lax.ppermute(x, AXES, pairs + [(b, a) for a, b in pairs])

    own = velocity.reshape(3, 8, 128)
    edge = exchange(own, [(i, i + 1) for i in range(PLANES - 1, total - 1, PLANES)])
    f_flat, base, local = relax(own, pressure.reshape(1, 8, 128), fields, brownian)
    near = lax.all_gather(jnp.stack([own, edge]), "field", axis=0)
    new_fields, kept, outer, inner = share(near, local, f_flat, base)

    outer = exchange(outer, [(i, i + PLANES) for i in range(total - PLANES) if i // PLANES % 2 == 1])
    couples = [[i, i + PLANES] for i in range(total) if i // PLANES % 2 == 0]
    both = lax.all_gather(inner, AXES, axis=0, axis_index_groups=couples)
    inner = jnp.where(lax.axis_index("mesh") % 2 == 1, both[0], both[1])
    parts = lax.all_to_all(kept + (outer + inner), "field", 0, 0, tiled=True)
    result = (parts[0] + parts[1]) + (parts[2] + parts[3])
    return new_fields.reshape(fields.shape), result.reshape(velocity.shape)


def solution(mesh):
    placed = (
        P(None, ("mesh", "field"), None),
        P(("mesh", "field"), None),
        P(None, "field", "mesh", None),
        P(None, "field", "mesh", None),
    )
    return jax.shard_map(
        body,
        mesh=mesh,
        in_specs=placed,
        out_specs=(P(None, "field", "mesh", None), P(None, ("mesh", "field"), None)),
        check_vma=False,
    )
```

```python
import functools

import jax
import jax.numpy as jnp
from jax import lax
from jax.experimental import pallas as pl
from jax.experimental.pallas import tpu as pltpu
from jax.sharding import PartitionSpec as P

f32 = jnp.float32
bf16 = jnp.bfloat16

NF = 256
TIME_STEP = 0.02
AXIAL = 400.0
TRANSVERSE = 40.0
MAX_STRETCH = 50.0
VISCOSITY = 40.0
WEISSENBERG = 0.5
NOISE = (0.02 / 0.5) ** 0.5
DIAGONAL = 1.0 / 0.02 + 2.0 * 400.0 + 4.0 * 40.0
SWEEPS = 4
INDEX = ((0, 1, 2), (1, 3, 4), (2, 4, 5))
DIAGONAL_PAIRS = (0, 3, 5)

PLANES = 4
BLOCKS = 8
UNROLL = 16
AXES = ("mesh", "field")


def lane_masks():
    lane = lax.broadcasted_iota(jnp.int32, (8, 128), 1)
    row = lax.broadcasted_iota(jnp.int32, (8, 128), 0)
    return dict(
        z_hi=(lane % 32) < 31,
        z_lo=(lane % 32) > 0,
        lane_hi=lane < 96,
        lane_lo=lane >= 32,
        row_hi=row < 7,
        row_lo=row > 0,
        channel=(row >= 2) & (row < 6),
    )


def shift_z(v, masks):
    plus = jnp.where(masks["z_hi"], pltpu.roll(v, 127, 1), 0.0)
    minus = jnp.where(masks["z_lo"], pltpu.roll(v, 1, 1), 0.0)
    return plus, minus


def shift_y(v, masks):
    ahead = pltpu.roll(v, 96, 1)
    behind = pltpu.roll(v, 32, 1)
    next_row = jnp.where(masks["row_hi"], pltpu.roll(ahead, 7, 0), 0.0)
    last_row = jnp.where(masks["row_lo"], pltpu.roll(behind, 1, 0), 0.0)
    return jnp.where(masks["lane_hi"], ahead, next_row), jnp.where(masks["lane_lo"], behind, last_row)


def slope_y(v, masks):
    plus, minus = shift_y(v, masks)
    return (plus - minus) * 0.5


def slope_z(v, masks):
    plus, minus = shift_z(v, masks)
    return (plus - minus) * 0.5


def around(v, masks):
    y_plus, y_minus = shift_y(v, masks)
    z_plus, z_minus = shift_z(v, masks)
    return (y_plus + y_minus) + (z_plus + z_minus)


def lanes_of(j):
    return pl.ds(pl.multiple_of(128 * j, 128), 128)


def loads(j, sources, buffers, sem):
    lanes = lanes_of(j)
    return [
        pltpu.make_async_copy(src.at[:, :, h, :, lanes], buf.at[:, :, pl.ds(4 * h, 4), lanes], sem.at[j, 2 * w + h])
        for w, (src, buf) in enumerate(zip(sources, buffers))
        for h in range(2)
    ]


def stores(j, buf, dst, sem):
    lanes = lanes_of(j)
    return [
        pltpu.make_async_copy(buf.at[:, :, pl.ds(4 * h, 4), lanes], dst.at[:, :, h, :, lanes], sem.at[j, h])
        for h in range(2)
    ]


def relax_kernel(velocity_hbm, pressure_hbm, f_hbm, b_hbm, f_ref, base_ref, local_ref, f_buf, b_buf, sem, local_sem):
    pairs = b_buf.shape[1]

    def begin(j, carry):
        for copy in loads(j, (f_hbm, b_hbm), (f_buf, b_buf), sem):
            copy.start()
        return carry

    lax.fori_loop(0, BLOCKS, begin, 0)
    own = (
        pltpu.make_async_copy(velocity_hbm, local_ref.at[pl.ds(0, 3)], local_sem.at[0]),
        pltpu.make_async_copy(pressure_hbm, local_ref.at[pl.ds(3, 1)], local_sem.at[1]),
    )
    for copy in own:
        copy.start()

    def block(j, carry):
        lanes = lanes_of(j)
        for copy in loads(j, (f_hbm, b_hbm), (f_buf, b_buf), sem):
            copy.wait()

        def some(i, inner):
            for u in range(UNROLL):
                n = i * UNROLL + u
                f = [f_buf[c, n, :, lanes].astype(f32) for c in range(3)]
                length_sq = f[0] * f[0] + f[1] * f[1] + f[2] * f[2]
                pull = TIME_STEP * MAX_STRETCH / (2.0 * WEISSENBERG) * pltpu.reciprocal(MAX_STRETCH - length_sq)
                kept = 1.0 - pull
                for c in range(3):
                    f_ref[c, n, :, lanes] = f[c]
                    base_ref[c, n, :, lanes] = kept * f[c] + NOISE * b_buf[c, n, :, lanes].astype(f32)
            return inner

        return lax.fori_loop(0, pairs // UNROLL, some, carry)

    lax.fori_loop(0, BLOCKS, block, 0)
    for copy in own:
        copy.wait()


def in_hbm(x):
    return pltpu.with_memory_space_constraint(x, pltpu.HBM)


def relax(velocity, pressure, fields, brownian):
    n = fields.shape[1] // 2
    split = (3, n, 2, PLANES, 1024)
    flat = (3, n, 8, 1024)
    vmem = pl.BlockSpec(memory_space=pltpu.VMEM)
    hbm = pl.BlockSpec(memory_space=pl.ANY)
    return pl.pallas_call(
        relax_kernel,
        out_shape=(
            jax.ShapeDtypeStruct(flat, f32),
            jax.ShapeDtypeStruct(flat, f32),
            jax.ShapeDtypeStruct((4, 8, 128), f32),
        ),
        in_specs=[hbm] * 4,
        out_specs=[vmem, vmem, vmem],
        scratch_shapes=[
            pltpu.VMEM(flat, bf16),
            pltpu.VMEM(flat, bf16),
            pltpu.SemaphoreType.DMA((BLOCKS, 4)),
            pltpu.SemaphoreType.DMA((2,)),
        ],
        compiler_params=pltpu.CompilerParams(vmem_limit_bytes=24 << 20),
        cost_estimate=pl.CostEstimate(flops=10_000_000, bytes_accessed=8_000_000, transcendentals=0),
    )(*(in_hbm(x) for x in (velocity, pressure, fields.reshape(split), brownian.reshape(split))))


def stretch(f, base, g):
    return [base[o] + (g[3 * o] * f[0] + g[3 * o + 1] * f[1] + g[3 * o + 2] * f[2]) for o in range(3)]


def share_kernel(
    slabs, near_ref, local_ref, f_ref, base_ref, nf_hbm, own_ref, outer_ref, inner_ref, n_buf, grad, sums, sem
):
    pairs = f_ref.shape[1]
    slab = lax.axis_index("mesh")
    mine = lax.axis_index("field")
    masks = lane_masks()

    planes = [(0, 1), (0, 0), (1, 0), (2, 0), (3, 0), (3, 1)]
    for q in range(PLANES):
        for a in range(3):
            before, centre, after = (near_ref[d, e, a] for d, e in planes[q : q + 3])
            slopes = ((after - before) * 0.5, slope_y(centre, masks), slope_z(centre, masks))
            for c in range(3):
                value = slopes[c] * TIME_STEP
                grad[3 * a + c, pl.ds(q, 8, stride=8), :] = value
                grad[3 * a + c, pl.ds(q + 4, 8, stride=8), :] = value

    def block(j, carry):
        rows = pl.ds(pl.multiple_of(8 * j, 8), 8)
        lanes = lanes_of(j)
        g = [grad[k, rows, :] for k in range(9)]

        def some(i, acc):
            for u in range(UNROLL):
                n = i * UNROLL + u
                f = [f_ref[c, n, :, lanes] for c in range(3)]
                a = stretch(f, [base_ref[o, n, :, lanes] for o in range(3)], g)
                for c in range(3):
                    n_buf[c, n, :, lanes] = a[c].astype(bf16)
                s = [x * x for x in a]
                r = pltpu.reciprocal(MAX_STRETCH - (s[0] + s[1] + s[2]))
                p0 = r * a[0]
                p1 = r * a[1]
                products = (r * s[0], p0 * a[1], p0 * a[2], r * s[1], p1 * a[2], r * s[2])
                acc = tuple(x + y for x, y in zip(acc, products))
            return acc

        acc = lax.fori_loop(0, pairs // UNROLL, some, tuple(jnp.zeros((8, 128), f32) for _ in range(6)))
        for k in range(6):
            sums[k, rows, :] = acc[k]
        for copy in stores(j, n_buf, nf_hbm, sem):
            copy.start()
        return carry

    lax.fori_loop(0, BLOCKS, block, 0)

    scale = VISCOSITY / WEISSENBERG / NF * MAX_STRETCH
    stress = []
    for k in range(6):
        rows = []
        for q in range(PLANES):
            total = sums[k, pl.ds(q, 8, stride=8), :] + sums[k, pl.ds(q + 4, 8, stride=8), :]
            total = total * scale
            if k in DIAGONAL_PAIRS:
                total = total - VISCOSITY / WEISSENBERG / 4
            rows.append(total)
        stress.append(rows)

    own = [mine == q for q in range(PLANES)]
    zero = jnp.zeros((8, 128), f32)
    pressure = [jnp.where(own[q], local_ref[3], 0.0) for q in range(PLANES)]
    start = [[jnp.where(own[q], local_ref[a], 0.0) for q in range(PLANES)] for a in range(3)]

    def at(values, q):
        return values[q] if 0 <= q < PLANES else None

    def add(x, y):
        return y if x is None else x if y is None else x + y

    def halfway(values, q):
        plus, minus = at(values, q + 1), at(values, q - 1)
        if plus is None:
            return None if minus is None else minus * -0.5
        return plus * 0.5 if minus is None else (plus - minus) * 0.5

    first = -(SWEEPS)
    count = PLANES + 2 * SWEEPS
    fluid = []
    for q in range(first, first + count):
        plane = slab * PLANES + q
        inside = (plane >= 0) & (plane < slabs * PLANES)
        wide = plane < slabs * PLANES // 2
        value = jnp.where(masks["channel"] | wide, 1.0 / DIAGONAL, 0.0)
        fluid.append(jnp.where(inside, value, 0.0))

    sources, currents = [], [{q: start[a][q] for q in range(PLANES)} for a in range(3)]
    for a in range(3):
        source = {}
        for q in range(-1, PLANES + 1):
            total = halfway(stress[INDEX[a][0]], q)
            if a == 0:
                total = total - halfway(pressure, q) if total is not None else None
            if 0 <= q < PLANES:
                inner = slope_y(stress[INDEX[a][1]][q], masks) + slope_z(stress[INDEX[a][2]][q], masks)
                if a == 1:
                    inner = inner - slope_y(pressure[q], masks)
                if a == 2:
                    inner = inner - slope_z(pressure[q], masks)
                total = total + inner + start[a][q] * (1.0 / TIME_STEP)
            source[q] = total
        sources.append(source)
    for sweep in range(SWEEPS):
        for a in range(3):
            current = currents[a]
            later = {}
            for q in range(-1 - sweep, PLANES + 1 + sweep):
                total = sources[a].get(q)
                along = add(current.get(q - 1), current.get(q + 1))
                if along is not None:
                    total = add(total, AXIAL * along)
                if q in current:
                    total = add(total, TRANSVERSE * around(current[q], masks))
                later[q] = total * fluid[q - first]
            currents[a] = later
    odd = slab % 2 == 1
    for a in range(3):
        for q in range(PLANES):
            before, after = currents[a][q - PLANES], currents[a][q + PLANES]
            own_ref[q, a] = currents[a][q]
            outer_ref[q, a] = jnp.where(odd, after, before)
            inner_ref[q, a] = jnp.where(odd, before, after)

    def end(j, carry):
        for copy in stores(j, n_buf, nf_hbm, sem):
            copy.wait()
        return carry

    lax.fori_loop(0, BLOCKS, end, 0)


def share(near, local, f_flat, base):
    n = f_flat.shape[1]
    slabs = lax.axis_size("mesh")
    vmem = pl.BlockSpec(memory_space=pltpu.VMEM)
    part = jax.ShapeDtypeStruct((PLANES, 3, 8, 128), f32)
    return pl.pallas_call(
        functools.partial(share_kernel, slabs),
        out_shape=(jax.ShapeDtypeStruct((3, n, 2, PLANES, 1024), bf16), part, part, part),
        in_specs=[vmem] * 4,
        out_specs=[pl.BlockSpec(memory_space=pl.ANY), vmem, vmem, vmem],
        scratch_shapes=[
            pltpu.VMEM((3, n, 8, 1024), bf16),
            pltpu.VMEM((9, 64, 128), f32),
            pltpu.VMEM((6, 64, 128), f32),
            pltpu.SemaphoreType.DMA((BLOCKS, 2)),
        ],
        compiler_params=pltpu.CompilerParams(vmem_limit_bytes=16 << 20),
        cost_estimate=pl.CostEstimate(flops=13_000_000, bytes_accessed=7_000_000, transcendentals=0),
    )(near, local, f_flat, base)


def body(velocity, pressure, fields, brownian):
    total = lax.axis_size("mesh") * PLANES

    def exchange(x, pairs):
        return lax.ppermute(x, AXES, pairs + [(b, a) for a, b in pairs])

    own = velocity.reshape(3, 8, 128)
    edge = exchange(own, [(i, i + 1) for i in range(PLANES - 1, total - 1, PLANES)])
    f_flat, base, local = relax(own, pressure.reshape(1, 8, 128), fields, brownian)
    near = lax.all_gather(jnp.stack([own, edge]), "field", axis=0)
    new_fields, kept, outer, inner = share(near, local, f_flat, base)

    outer = exchange(outer, [(i, i + PLANES) for i in range(total - PLANES) if i // PLANES % 2 == 1])
    couples = [[i, i + PLANES] for i in range(total) if i // PLANES % 2 == 0]
    both = lax.all_gather(inner, AXES, axis=0, axis_index_groups=couples)
    inner = jnp.where(lax.axis_index("mesh") % 2 == 1, both[0], both[1])
    parts = lax.all_gather(kept + (outer + inner), "field", axis=0)
    parts = lax.dynamic_index_in_dim(parts, lax.axis_index("field"), 1, keepdims=False)
    result = (parts[0] + parts[1]) + (parts[2] + parts[3])
    return new_fields.reshape(fields.shape), result.reshape(velocity.shape)


def solution(mesh):
    placed = (
        P(None, ("mesh", "field"), None),
        P(("mesh", "field"), None),
        P(None, "field", "mesh", None),
        P(None, "field", "mesh", None),
    )
    return jax.shard_map(
        body,
        mesh=mesh,
        in_specs=placed,
        out_specs=(P(None, "field", "mesh", None), P(None, ("mesh", "field"), None)),
        check_vma=False,
    )
```

```python
import functools

import jax
import jax.numpy as jnp
from jax import lax
from jax.experimental import pallas as pl
from jax.experimental.pallas import tpu as pltpu
from jax.sharding import PartitionSpec as P

f32 = jnp.float32
bf16 = jnp.bfloat16

NF = 256
TIME_STEP = 0.02
AXIAL = 400.0
TRANSVERSE = 40.0
MAX_STRETCH = 50.0
VISCOSITY = 40.0
WEISSENBERG = 0.5
NOISE = (0.02 / 0.5) ** 0.5
DIAGONAL = 1.0 / 0.02 + 2.0 * 400.0 + 4.0 * 40.0
SWEEPS = 4
INDEX = ((0, 1, 2), (1, 3, 4), (2, 4, 5))
DIAGONAL_PAIRS = (0, 3, 5)

PLANES = 4
BLOCKS = 8
UNROLL = 16
AXES = ("mesh", "field")


def lane_masks():
    lane = lax.broadcasted_iota(jnp.int32, (8, 128), 1)
    row = lax.broadcasted_iota(jnp.int32, (8, 128), 0)
    return dict(
        z_hi=(lane % 32) < 31,
        z_lo=(lane % 32) > 0,
        lane_hi=lane < 96,
        lane_lo=lane >= 32,
        row_hi=row < 7,
        row_lo=row > 0,
        channel=(row >= 2) & (row < 6),
    )


def shift_z(v, masks):
    plus = jnp.where(masks["z_hi"], pltpu.roll(v, 127, 1), 0.0)
    minus = jnp.where(masks["z_lo"], pltpu.roll(v, 1, 1), 0.0)
    return plus, minus


def shift_y(v, masks):
    ahead = pltpu.roll(v, 96, 1)
    behind = pltpu.roll(v, 32, 1)
    next_row = jnp.where(masks["row_hi"], pltpu.roll(ahead, 7, 0), 0.0)
    last_row = jnp.where(masks["row_lo"], pltpu.roll(behind, 1, 0), 0.0)
    return jnp.where(masks["lane_hi"], ahead, next_row), jnp.where(masks["lane_lo"], behind, last_row)


def slope_y(v, masks):
    plus, minus = shift_y(v, masks)
    return (plus - minus) * 0.5


def slope_z(v, masks):
    plus, minus = shift_z(v, masks)
    return (plus - minus) * 0.5


def around(v, masks):
    y_plus, y_minus = shift_y(v, masks)
    z_plus, z_minus = shift_z(v, masks)
    return (y_plus + y_minus) + (z_plus + z_minus)


def lanes_of(j):
    return pl.ds(pl.multiple_of(128 * j, 128), 128)


def loads(j, sources, buffers, sem):
    lanes = lanes_of(j)
    return [
        pltpu.make_async_copy(src.at[:, :, h, :, lanes], buf.at[:, :, pl.ds(4 * h, 4), lanes], sem.at[j, 2 * w + h])
        for w, (src, buf) in enumerate(zip(sources, buffers))
        for h in range(2)
    ]


def stores(j, buf, dst, sem):
    lanes = lanes_of(j)
    return [
        pltpu.make_async_copy(buf.at[:, :, pl.ds(4 * h, 4), lanes], dst.at[:, :, h, :, lanes], sem.at[j, h])
        for h in range(2)
    ]


def relax_kernel(velocity_hbm, pressure_hbm, f_hbm, b_hbm, f_ref, base_ref, local_ref, f_buf, b_buf, sem, local_sem):
    pairs = b_buf.shape[1]

    def begin(j, carry):
        for copy in loads(j, (f_hbm, b_hbm), (f_buf, b_buf), sem):
            copy.start()
        return carry

    lax.fori_loop(0, BLOCKS, begin, 0)
    own = (
        pltpu.make_async_copy(velocity_hbm, local_ref.at[pl.ds(0, 3)], local_sem.at[0]),
        pltpu.make_async_copy(pressure_hbm, local_ref.at[pl.ds(3, 1)], local_sem.at[1]),
    )
    for copy in own:
        copy.start()

    def block(j, carry):
        lanes = lanes_of(j)
        for copy in loads(j, (f_hbm, b_hbm), (f_buf, b_buf), sem):
            copy.wait()

        def some(i, inner):
            for u in range(UNROLL):
                n = i * UNROLL + u
                f = [f_buf[c, n, :, lanes].astype(f32) for c in range(3)]
                length_sq = f[0] * f[0] + f[1] * f[1] + f[2] * f[2]
                pull = TIME_STEP * MAX_STRETCH / (2.0 * WEISSENBERG) * pltpu.reciprocal(MAX_STRETCH - length_sq)
                kept = 1.0 - pull
                for c in range(3):
                    f_ref[c, n, :, lanes] = f[c]
                    base_ref[c, n, :, lanes] = kept * f[c] + NOISE * b_buf[c, n, :, lanes].astype(f32)
            return inner

        return lax.fori_loop(0, pairs // UNROLL, some, carry)

    lax.fori_loop(0, BLOCKS, block, 0)
    for copy in own:
        copy.wait()


def in_hbm(x):
    return pltpu.with_memory_space_constraint(x, pltpu.HBM)


def relax(velocity, pressure, fields, brownian):
    n = fields.shape[1] // 2
    split = (3, n, 2, PLANES, 1024)
    flat = (3, n, 8, 1024)
    vmem = pl.BlockSpec(memory_space=pltpu.VMEM)
    hbm = pl.BlockSpec(memory_space=pl.ANY)
    return pl.pallas_call(
        relax_kernel,
        out_shape=(
            jax.ShapeDtypeStruct(flat, f32),
            jax.ShapeDtypeStruct(flat, f32),
            jax.ShapeDtypeStruct((4, 8, 128), f32),
        ),
        in_specs=[hbm] * 4,
        out_specs=[vmem, vmem, vmem],
        scratch_shapes=[
            pltpu.VMEM(flat, bf16),
            pltpu.VMEM(flat, bf16),
            pltpu.SemaphoreType.DMA((BLOCKS, 4)),
            pltpu.SemaphoreType.DMA((2,)),
        ],
        compiler_params=pltpu.CompilerParams(vmem_limit_bytes=24 << 20),
        cost_estimate=pl.CostEstimate(flops=10_000_000, bytes_accessed=8_000_000, transcendentals=0),
    )(*(in_hbm(x) for x in (velocity, pressure, fields.reshape(split), brownian.reshape(split))))


def stretch(f, base, g):
    return [base[o] + (g[3 * o] * f[0] + g[3 * o + 1] * f[1] + g[3 * o + 2] * f[2]) for o in range(3)]


def share_kernel(
    slabs, near_ref, local_ref, f_ref, base_ref, nf_hbm, own_ref, outer_ref, inner_ref, n_buf, grad, sums, sem
):
    pairs = f_ref.shape[1]
    slab = lax.axis_index("mesh")
    mine = lax.axis_index("field")
    masks = lane_masks()

    planes = [(1, 1), (0, 0), (1, 0), (2, 0), (3, 0), (3, 1)]
    for q in range(PLANES):
        for a in range(3):
            before, centre, after = (near_ref[d, e, a] for d, e in planes[q : q + 3])
            slopes = ((after - before) * 0.5, slope_y(centre, masks), slope_z(centre, masks))
            for c in range(3):
                value = slopes[c] * TIME_STEP
                grad[3 * a + c, pl.ds(q, 8, stride=8), :] = value
                grad[3 * a + c, pl.ds(q + 4, 8, stride=8), :] = value

    def block(j, carry):
        rows = pl.ds(pl.multiple_of(8 * j, 8), 8)
        lanes = lanes_of(j)
        g = [grad[k, rows, :] for k in range(9)]

        def some(i, acc):
            for u in range(UNROLL):
                n = i * UNROLL + u
                f = [f_ref[c, n, :, lanes] for c in range(3)]
                a = stretch(f, [base_ref[o, n, :, lanes] for o in range(3)], g)
                for c in range(3):
                    n_buf[c, n, :, lanes] = a[c].astype(bf16)
                s = [x * x for x in a]
                r = pltpu.reciprocal(MAX_STRETCH - (s[0] + s[1] + s[2]))
                p0 = r * a[0]
                p1 = r * a[1]
                products = (r * s[0], p0 * a[1], p0 * a[2], r * s[1], p1 * a[2], r * s[2])
                acc = tuple(x + y for x, y in zip(acc, products))
            return acc

        acc = lax.fori_loop(0, pairs // UNROLL, some, tuple(jnp.zeros((8, 128), f32) for _ in range(6)))
        for k in range(6):
            sums[k, rows, :] = acc[k]
        for copy in stores(j, n_buf, nf_hbm, sem):
            copy.start()
        return carry

    lax.fori_loop(0, BLOCKS, block, 0)

    scale = VISCOSITY / WEISSENBERG / NF * MAX_STRETCH
    stress = []
    for k in range(6):
        rows = []
        for q in range(PLANES):
            total = sums[k, pl.ds(q, 8, stride=8), :] + sums[k, pl.ds(q + 4, 8, stride=8), :]
            total = total * scale
            if k in DIAGONAL_PAIRS:
                total = total - VISCOSITY / WEISSENBERG / 4
            rows.append(total)
        stress.append(rows)

    own = [mine == q for q in range(PLANES)]
    zero = jnp.zeros((8, 128), f32)
    pressure = [jnp.where(own[q], local_ref[3], 0.0) for q in range(PLANES)]
    start = [[jnp.where(own[q], local_ref[a], 0.0) for q in range(PLANES)] for a in range(3)]

    def at(values, q):
        return values[q] if 0 <= q < PLANES else None

    def add(x, y):
        return y if x is None else x if y is None else x + y

    def halfway(values, q):
        plus, minus = at(values, q + 1), at(values, q - 1)
        if plus is None:
            return None if minus is None else minus * -0.5
        return plus * 0.5 if minus is None else (plus - minus) * 0.5

    first = -(SWEEPS)
    count = PLANES + 2 * SWEEPS
    fluid = []
    for q in range(first, first + count):
        plane = slab * PLANES + q
        inside = (plane >= 0) & (plane < slabs * PLANES)
        wide = plane < slabs * PLANES // 2
        value = jnp.where(masks["channel"] | wide, 1.0 / DIAGONAL, 0.0)
        fluid.append(jnp.where(inside, value, 0.0))

    sources, currents = [], [{q: start[a][q] for q in range(PLANES)} for a in range(3)]
    for a in range(3):
        source = {}
        for q in range(-1, PLANES + 1):
            total = halfway(stress[INDEX[a][0]], q)
            if a == 0:
                total = total - halfway(pressure, q) if total is not None else None
            if 0 <= q < PLANES:
                inner = slope_y(stress[INDEX[a][1]][q], masks) + slope_z(stress[INDEX[a][2]][q], masks)
                if a == 1:
                    inner = inner - slope_y(pressure[q], masks)
                if a == 2:
                    inner = inner - slope_z(pressure[q], masks)
                total = total + inner + start[a][q] * (1.0 / TIME_STEP)
            source[q] = total
        sources.append(source)
    for sweep in range(SWEEPS):
        for a in range(3):
            current = currents[a]
            later = {}
            for q in range(-1 - sweep, PLANES + 1 + sweep):
                total = sources[a].get(q)
                along = add(current.get(q - 1), current.get(q + 1))
                if along is not None:
                    total = add(total, AXIAL * along)
                if q in current:
                    total = add(total, TRANSVERSE * around(current[q], masks))
                later[q] = total * fluid[q - first]
            currents[a] = later
    odd = slab % 2 == 1
    for a in range(3):
        for q in range(PLANES):
            before, after = currents[a][q - PLANES], currents[a][q + PLANES]
            own_ref[q, a] = currents[a][q]
            outer_ref[q, a] = jnp.where(odd, after, before)
            inner_ref[q, a] = jnp.where(odd, before, after)

    def end(j, carry):
        for copy in stores(j, n_buf, nf_hbm, sem):
            copy.wait()
        return carry

    lax.fori_loop(0, BLOCKS, end, 0)


def share(near, local, f_flat, base):
    n = f_flat.shape[1]
    slabs = lax.axis_size("mesh")
    vmem = pl.BlockSpec(memory_space=pltpu.VMEM)
    part = jax.ShapeDtypeStruct((PLANES, 3, 8, 128), f32)
    return pl.pallas_call(
        functools.partial(share_kernel, slabs),
        out_shape=(jax.ShapeDtypeStruct((3, n, 2, PLANES, 1024), bf16), part, part, part),
        in_specs=[vmem] * 4,
        out_specs=[pl.BlockSpec(memory_space=pl.ANY), vmem, vmem, vmem],
        scratch_shapes=[
            pltpu.VMEM((3, n, 8, 1024), bf16),
            pltpu.VMEM((9, 64, 128), f32),
            pltpu.VMEM((6, 64, 128), f32),
            pltpu.SemaphoreType.DMA((BLOCKS, 2)),
        ],
        compiler_params=pltpu.CompilerParams(vmem_limit_bytes=16 << 20),
        cost_estimate=pl.CostEstimate(flops=13_000_000, bytes_accessed=7_000_000, transcendentals=0),
    )(near, local, f_flat, base)


def body(velocity, pressure, fields, brownian):
    total = lax.axis_size("mesh") * PLANES

    def exchange(x, pairs):
        return lax.ppermute(x, AXES, pairs + [(b, a) for a, b in pairs])

    own = velocity.reshape(3, 8, 128)
    ends = range(PLANES - 1, total - 1, PLANES)
    edge = lax.ppermute(own, AXES, [(i, i + 2) for i in ends] + [(i + 1, i) for i in ends])
    f_flat, base, local = relax(own, pressure.reshape(1, 8, 128), fields, brownian)
    near = lax.all_gather(jnp.stack([own, edge]), "field", axis=0)
    new_fields, kept, outer, inner = share(near, local, f_flat, base)

    outer = exchange(outer, [(i, i + PLANES) for i in range(total - PLANES) if i // PLANES % 2 == 1])
    couples = [[i, i + PLANES] for i in range(total) if i // PLANES % 2 == 0]
    both = lax.all_gather(inner, AXES, axis=0, axis_index_groups=couples)
    inner = jnp.where(lax.axis_index("mesh") % 2 == 1, both[0], both[1])
    parts = lax.all_gather(kept + (outer + inner), "field", axis=0)
    parts = lax.dynamic_index_in_dim(parts, lax.axis_index("field"), 1, keepdims=False)
    result = (parts[0] + parts[1]) + (parts[2] + parts[3])
    return new_fields.reshape(fields.shape), result.reshape(velocity.shape)


def solution(mesh):
    placed = (
        P(None, ("mesh", "field"), None),
        P(("mesh", "field"), None),
        P(None, "field", "mesh", None),
        P(None, "field", "mesh", None),
    )
    return jax.shard_map(
        body,
        mesh=mesh,
        in_specs=placed,
        out_specs=(P(None, "field", "mesh", None), P(None, ("mesh", "field"), None)),
        check_vma=False,
    )
```

```python
import functools

import jax
import jax.numpy as jnp
from jax import lax
from jax.experimental import pallas as pl
from jax.experimental.pallas import tpu as pltpu
from jax.sharding import PartitionSpec as P

f32 = jnp.float32
bf16 = jnp.bfloat16

NF = 256
TIME_STEP = 0.02
AXIAL = 400.0
TRANSVERSE = 40.0
MAX_STRETCH = 50.0
VISCOSITY = 40.0
WEISSENBERG = 0.5
NOISE = (0.02 / 0.5) ** 0.5
DIAGONAL = 1.0 / 0.02 + 2.0 * 400.0 + 4.0 * 40.0
SWEEPS = 4
INDEX = ((0, 1, 2), (1, 3, 4), (2, 4, 5))
DIAGONAL_PAIRS = (0, 3, 5)

PLANES = 4
BLOCKS = 8
UNROLL = 16
AXES = ("mesh", "field")


def lane_masks():
    lane = lax.broadcasted_iota(jnp.int32, (8, 128), 1)
    row = lax.broadcasted_iota(jnp.int32, (8, 128), 0)
    return dict(
        z_hi=(lane % 32) < 31,
        z_lo=(lane % 32) > 0,
        lane_hi=lane < 96,
        lane_lo=lane >= 32,
        row_hi=row < 7,
        row_lo=row > 0,
        channel=(row >= 2) & (row < 6),
    )


def shift_z(v, masks):
    plus = jnp.where(masks["z_hi"], pltpu.roll(v, 127, 1), 0.0)
    minus = jnp.where(masks["z_lo"], pltpu.roll(v, 1, 1), 0.0)
    return plus, minus


def shift_y(v, masks):
    ahead = pltpu.roll(v, 96, 1)
    behind = pltpu.roll(v, 32, 1)
    next_row = jnp.where(masks["row_hi"], pltpu.roll(ahead, 7, 0), 0.0)
    last_row = jnp.where(masks["row_lo"], pltpu.roll(behind, 1, 0), 0.0)
    return jnp.where(masks["lane_hi"], ahead, next_row), jnp.where(masks["lane_lo"], behind, last_row)


def slope_y(v, masks):
    plus, minus = shift_y(v, masks)
    return (plus - minus) * 0.5


def slope_z(v, masks):
    plus, minus = shift_z(v, masks)
    return (plus - minus) * 0.5


def around(v, masks):
    y_plus, y_minus = shift_y(v, masks)
    z_plus, z_minus = shift_z(v, masks)
    return (y_plus + y_minus) + (z_plus + z_minus)


def lanes_of(j):
    return pl.ds(pl.multiple_of(128 * j, 128), 128)


def loads(j, sources, buffers, sem):
    lanes = lanes_of(j)
    return [
        pltpu.make_async_copy(src.at[:, :, h, :, lanes], buf.at[:, :, pl.ds(4 * h, 4), lanes], sem.at[j, 2 * w + h])
        for w, (src, buf) in enumerate(zip(sources, buffers))
        for h in range(2)
    ]


def stores(j, buf, dst, sem):
    lanes = lanes_of(j)
    return [
        pltpu.make_async_copy(buf.at[:, :, pl.ds(4 * h, 4), lanes], dst.at[:, :, h, :, lanes], sem.at[j, h])
        for h in range(2)
    ]


def relax_kernel(velocity_hbm, pressure_hbm, f_hbm, b_hbm, f_ref, base_ref, local_ref, f_buf, b_buf, sem, local_sem):
    pairs = b_buf.shape[1]

    def begin(j, carry):
        for copy in loads(j, (f_hbm, b_hbm), (f_buf, b_buf), sem):
            copy.start()
        return carry

    lax.fori_loop(0, BLOCKS, begin, 0)
    own = (
        pltpu.make_async_copy(velocity_hbm, local_ref.at[pl.ds(0, 3)], local_sem.at[0]),
        pltpu.make_async_copy(pressure_hbm, local_ref.at[pl.ds(3, 1)], local_sem.at[1]),
    )
    for copy in own:
        copy.start()

    def block(j, carry):
        lanes = lanes_of(j)
        for copy in loads(j, (f_hbm, b_hbm), (f_buf, b_buf), sem):
            copy.wait()

        def some(i, inner):
            for u in range(UNROLL):
                n = i * UNROLL + u
                f = [f_buf[c, n, :, lanes].astype(f32) for c in range(3)]
                length_sq = f[0] * f[0] + f[1] * f[1] + f[2] * f[2]
                pull = TIME_STEP * MAX_STRETCH / (2.0 * WEISSENBERG) * pltpu.reciprocal(MAX_STRETCH - length_sq)
                kept = 1.0 - pull
                for c in range(3):
                    f_ref[c, n, :, lanes] = f[c]
                    base_ref[c, n, :, lanes] = kept * f[c] + NOISE * b_buf[c, n, :, lanes].astype(f32)
            return inner

        return lax.fori_loop(0, pairs // UNROLL, some, carry)

    lax.fori_loop(0, BLOCKS, block, 0)
    for copy in own:
        copy.wait()


def in_hbm(x):
    return pltpu.with_memory_space_constraint(x, pltpu.HBM)


def relax(velocity, pressure, fields, brownian):
    n = fields.shape[1] // 2
    split = (3, n, 2, PLANES, 1024)
    flat = (3, n, 8, 1024)
    vmem = pl.BlockSpec(memory_space=pltpu.VMEM)
    hbm = pl.BlockSpec(memory_space=pl.ANY)
    return pl.pallas_call(
        relax_kernel,
        out_shape=(
            jax.ShapeDtypeStruct(flat, f32),
            jax.ShapeDtypeStruct(flat, f32),
            jax.ShapeDtypeStruct((4, 8, 128), f32),
        ),
        in_specs=[hbm] * 4,
        out_specs=[vmem, vmem, vmem],
        scratch_shapes=[
            pltpu.VMEM(flat, bf16),
            pltpu.VMEM(flat, bf16),
            pltpu.SemaphoreType.DMA((BLOCKS, 4)),
            pltpu.SemaphoreType.DMA((2,)),
        ],
        compiler_params=pltpu.CompilerParams(vmem_limit_bytes=24 << 20),
        cost_estimate=pl.CostEstimate(flops=10_000_000, bytes_accessed=8_000_000, transcendentals=0),
    )(*(in_hbm(x) for x in (velocity, pressure, fields.reshape(split), brownian.reshape(split))))


def stretch(f, base, g):
    return [base[o] + (g[3 * o] * f[0] + g[3 * o + 1] * f[1] + g[3 * o + 2] * f[2]) for o in range(3)]


def share_kernel(
    slabs, near_ref, local_ref, f_ref, base_ref, nf_hbm, own_ref, outer_ref, inner_ref, n_buf, grad, sums, sem
):
    pairs = f_ref.shape[1]
    slab = lax.axis_index("mesh")
    mine = lax.axis_index("field")
    masks = lane_masks()

    planes = [(1, 1), (0, 0), (1, 0), (2, 0), (3, 0), (3, 1)]
    for q in range(PLANES):
        for a in range(3):
            before, centre, after = (near_ref[d, e, a] for d, e in planes[q : q + 3])
            slopes = ((after - before) * 0.5, slope_y(centre, masks), slope_z(centre, masks))
            for c in range(3):
                value = slopes[c] * TIME_STEP
                grad[3 * a + c, pl.ds(q, 8, stride=8), :] = value
                grad[3 * a + c, pl.ds(q + 4, 8, stride=8), :] = value

    def block(j, carry):
        rows = pl.ds(pl.multiple_of(8 * j, 8), 8)
        lanes = lanes_of(j)
        g = [grad[k, rows, :] for k in range(9)]

        def some(i, acc):
            for u in range(UNROLL):
                n = i * UNROLL + u
                f = [f_ref[c, n, :, lanes] for c in range(3)]
                a = stretch(f, [base_ref[o, n, :, lanes] for o in range(3)], g)
                for c in range(3):
                    n_buf[c, n, :, lanes] = a[c].astype(bf16)
                s = [x * x for x in a]
                r = pltpu.reciprocal(MAX_STRETCH - (s[0] + s[1] + s[2]))
                p0 = r * a[0]
                p1 = r * a[1]
                products = (r * s[0], p0 * a[1], p0 * a[2], r * s[1], p1 * a[2], r * s[2])
                acc = tuple(x + y for x, y in zip(acc, products))
            return acc

        acc = lax.fori_loop(0, pairs // UNROLL, some, tuple(jnp.zeros((8, 128), f32) for _ in range(6)))
        for k in range(6):
            sums[k, rows, :] = acc[k]
        for copy in stores(j, n_buf, nf_hbm, sem):
            copy.start()
        return carry

    lax.fori_loop(0, BLOCKS, block, 0)

    scale = VISCOSITY / WEISSENBERG / NF * MAX_STRETCH
    stress = []
    for k in range(6):
        rows = []
        for q in range(PLANES):
            total = sums[k, pl.ds(q, 8, stride=8), :] + sums[k, pl.ds(q + 4, 8, stride=8), :]
            total = total * scale
            if k in DIAGONAL_PAIRS:
                total = total - VISCOSITY / WEISSENBERG / 4
            rows.append(total)
        stress.append(rows)

    own = [mine == q for q in range(PLANES)]
    zero = jnp.zeros((8, 128), f32)
    pressure = [jnp.where(own[q], local_ref[3], 0.0) for q in range(PLANES)]
    start = [[jnp.where(own[q], local_ref[a], 0.0) for q in range(PLANES)] for a in range(3)]

    def at(values, q):
        return values[q] if 0 <= q < PLANES else None

    def add(x, y):
        return y if x is None else x if y is None else x + y

    def halfway(values, q):
        plus, minus = at(values, q + 1), at(values, q - 1)
        if plus is None:
            return None if minus is None else minus * -0.5
        return plus * 0.5 if minus is None else (plus - minus) * 0.5

    first = -(SWEEPS)
    count = PLANES + 2 * SWEEPS
    fluid = []
    for q in range(first, first + count):
        plane = slab * PLANES + q
        inside = (plane >= 0) & (plane < slabs * PLANES)
        wide = plane < slabs * PLANES // 2
        value = jnp.where(masks["channel"] | wide, 1.0 / DIAGONAL, 0.0)
        fluid.append(jnp.where(inside, value, 0.0))

    sources, currents = [], [{q: start[a][q] for q in range(PLANES)} for a in range(3)]
    for a in range(3):
        source = {}
        for q in range(-1, PLANES + 1):
            total = halfway(stress[INDEX[a][0]], q)
            if a == 0:
                total = total - halfway(pressure, q) if total is not None else None
            if 0 <= q < PLANES:
                inner = slope_y(stress[INDEX[a][1]][q], masks) + slope_z(stress[INDEX[a][2]][q], masks)
                if a == 1:
                    inner = inner - slope_y(pressure[q], masks)
                if a == 2:
                    inner = inner - slope_z(pressure[q], masks)
                total = total + inner + start[a][q] * (1.0 / TIME_STEP)
            source[q] = total
        sources.append(source)
    for sweep in range(SWEEPS):
        for a in range(3):
            current = currents[a]
            later = {}
            for q in range(-1 - sweep, PLANES + 1 + sweep):
                total = sources[a].get(q)
                along = add(current.get(q - 1), current.get(q + 1))
                if along is not None:
                    total = add(total, AXIAL * along)
                if q in current:
                    total = add(total, TRANSVERSE * around(current[q], masks))
                later[q] = total * fluid[q - first]
            currents[a] = later
    odd = slab % 2 == 1
    for a in range(3):
        for q in range(PLANES):
            before, after = currents[a][q - PLANES], currents[a][q + PLANES]
            own_ref[q, a] = currents[a][q]
            outer_ref[q, a] = jnp.where(odd, after, before)
            inner_ref[q, a] = jnp.where(odd, before, after)

    def end(j, carry):
        for copy in stores(j, n_buf, nf_hbm, sem):
            copy.wait()
        return carry

    lax.fori_loop(0, BLOCKS, end, 0)


def share(near, local, f_flat, base):
    n = f_flat.shape[1]
    slabs = lax.axis_size("mesh")
    vmem = pl.BlockSpec(memory_space=pltpu.VMEM)
    part = jax.ShapeDtypeStruct((PLANES, 3, 8, 128), f32)
    return pl.pallas_call(
        functools.partial(share_kernel, slabs),
        out_shape=(jax.ShapeDtypeStruct((3, n, 2, PLANES, 1024), bf16), part, part, part),
        in_specs=[vmem] * 4,
        out_specs=[pl.BlockSpec(memory_space=pl.ANY), vmem, vmem, vmem],
        scratch_shapes=[
            pltpu.VMEM((3, n, 8, 1024), bf16),
            pltpu.VMEM((9, 64, 128), f32),
            pltpu.VMEM((6, 64, 128), f32),
            pltpu.SemaphoreType.DMA((BLOCKS, 2)),
        ],
        compiler_params=pltpu.CompilerParams(vmem_limit_bytes=16 << 20),
        cost_estimate=pl.CostEstimate(flops=13_000_000, bytes_accessed=7_000_000, transcendentals=0),
    )(near, local, f_flat, base)


def body(velocity, pressure, fields, brownian):
    total = lax.axis_size("mesh") * PLANES

    def exchange(x, pairs):
        return lax.ppermute(x, AXES, pairs + [(b, a) for a, b in pairs])

    own = velocity.reshape(3, 8, 128)
    ends = range(PLANES - 1, total - 1, PLANES)
    edge = lax.ppermute(own, AXES, [(i, i + 2) for i in ends] + [(i + 1, i) for i in ends])
    f_flat, base, local = relax(own, pressure.reshape(1, 8, 128), fields, brownian)
    near = lax.all_gather(jnp.stack([own, edge]), "field", axis=0)
    new_fields, kept, outer, inner = share(near, local, f_flat, base)

    outer = exchange(outer, [(i, (i + PLANES) ^ 1) for i in range(total - PLANES) if i // PLANES % 2 == 1])
    couples = [[i, i + PLANES] for i in range(total) if i // PLANES % 2 == 0]
    both = lax.all_gather(inner, AXES, axis=0, axis_index_groups=couples)
    inner = jnp.where(lax.axis_index("mesh") % 2 == 1, both[0], both[1])
    parts = lax.all_gather(kept + (outer + inner), "field", axis=0)
    parts = lax.dynamic_index_in_dim(parts, lax.axis_index("field"), 1, keepdims=False)
    result = (parts[0] + parts[1]) + (parts[2] + parts[3])
    return new_fields.reshape(fields.shape), result.reshape(velocity.shape)


def solution(mesh):
    placed = (
        P(None, ("mesh", "field"), None),
        P(("mesh", "field"), None),
        P(None, "field", "mesh", None),
        P(None, "field", "mesh", None),
    )
    return jax.shard_map(
        body,
        mesh=mesh,
        in_specs=placed,
        out_specs=(P(None, "field", "mesh", None), P(None, ("mesh", "field"), None)),
        check_vma=False,
    )
```

```python
import functools

import jax
import jax.numpy as jnp
from jax import lax
from jax.experimental import pallas as pl
from jax.experimental.pallas import tpu as pltpu
from jax.sharding import PartitionSpec as P

f32 = jnp.float32
bf16 = jnp.bfloat16

NF = 256
TIME_STEP = 0.02
AXIAL = 400.0
TRANSVERSE = 40.0
MAX_STRETCH = 50.0
VISCOSITY = 40.0
WEISSENBERG = 0.5
NOISE = (0.02 / 0.5) ** 0.5
DIAGONAL = 1.0 / 0.02 + 2.0 * 400.0 + 4.0 * 40.0
SWEEPS = 4
INDEX = ((0, 1, 2), (1, 3, 4), (2, 4, 5))
DIAGONAL_PAIRS = (0, 3, 5)

PLANES = 4
BLOCKS = 8
UNROLL = 16
AXES = ("mesh", "field")


def lane_masks():
    lane = lax.broadcasted_iota(jnp.int32, (8, 128), 1)
    row = lax.broadcasted_iota(jnp.int32, (8, 128), 0)
    return dict(
        z_hi=(lane % 32) < 31,
        z_lo=(lane % 32) > 0,
        lane_hi=lane < 96,
        lane_lo=lane >= 32,
        row_hi=row < 7,
        row_lo=row > 0,
        channel=(row >= 2) & (row < 6),
    )


def shift_z(v, masks):
    plus = jnp.where(masks["z_hi"], pltpu.roll(v, 127, 1), 0.0)
    minus = jnp.where(masks["z_lo"], pltpu.roll(v, 1, 1), 0.0)
    return plus, minus


def shift_y(v, masks):
    ahead = pltpu.roll(v, 96, 1)
    behind = pltpu.roll(v, 32, 1)
    next_row = jnp.where(masks["row_hi"], pltpu.roll(ahead, 7, 0), 0.0)
    last_row = jnp.where(masks["row_lo"], pltpu.roll(behind, 1, 0), 0.0)
    return jnp.where(masks["lane_hi"], ahead, next_row), jnp.where(masks["lane_lo"], behind, last_row)


def slope_y(v, masks):
    plus, minus = shift_y(v, masks)
    return (plus - minus) * 0.5


def slope_z(v, masks):
    plus, minus = shift_z(v, masks)
    return (plus - minus) * 0.5


def around(v, masks):
    y_plus, y_minus = shift_y(v, masks)
    z_plus, z_minus = shift_z(v, masks)
    return (y_plus + y_minus) + (z_plus + z_minus)


def lanes_of(j):
    return pl.ds(pl.multiple_of(128 * j, 128), 128)


def loads(j, sources, buffers, sem):
    lanes = lanes_of(j)
    return [
        pltpu.make_async_copy(src.at[:, :, h, :, lanes], buf.at[:, :, pl.ds(4 * h, 4), lanes], sem.at[j, 2 * w + h])
        for w, (src, buf) in enumerate(zip(sources, buffers))
        for h in range(2)
    ]


def stores(j, buf, dst, sem):
    lanes = lanes_of(j)
    return [
        pltpu.make_async_copy(buf.at[:, :, pl.ds(4 * h, 4), lanes], dst.at[:, :, h, :, lanes], sem.at[j, h])
        for h in range(2)
    ]


def relax_kernel(velocity_hbm, pressure_hbm, f_hbm, b_hbm, f_ref, base_ref, local_ref, f_buf, b_buf, sem, local_sem):
    pairs = b_buf.shape[1]

    def begin(j, carry):
        for copy in loads(j, (f_hbm, b_hbm), (f_buf, b_buf), sem):
            copy.start()
        return carry

    lax.fori_loop(0, BLOCKS, begin, 0)
    own = (
        pltpu.make_async_copy(velocity_hbm, local_ref.at[pl.ds(0, 3)], local_sem.at[0]),
        pltpu.make_async_copy(pressure_hbm, local_ref.at[pl.ds(3, 1)], local_sem.at[1]),
    )
    for copy in own:
        copy.start()

    def block(j, carry):
        lanes = lanes_of(j)
        for copy in loads(j, (f_hbm, b_hbm), (f_buf, b_buf), sem):
            copy.wait()

        def some(i, inner):
            for u in range(UNROLL):
                n = i * UNROLL + u
                f = [f_buf[c, n, :, lanes].astype(f32) for c in range(3)]
                length_sq = f[0] * f[0] + f[1] * f[1] + f[2] * f[2]
                pull = TIME_STEP * MAX_STRETCH / (2.0 * WEISSENBERG) * pltpu.reciprocal(MAX_STRETCH - length_sq)
                kept = 1.0 - pull
                for c in range(3):
                    f_ref[c, n, :, lanes] = f[c]
                    base_ref[c, n, :, lanes] = kept * f[c] + NOISE * b_buf[c, n, :, lanes].astype(f32)
            return inner

        return lax.fori_loop(0, pairs // UNROLL, some, carry)

    lax.fori_loop(0, BLOCKS, block, 0)
    for copy in own:
        copy.wait()


def in_hbm(x):
    return pltpu.with_memory_space_constraint(x, pltpu.HBM)


def relax(velocity, pressure, fields, brownian):
    n = fields.shape[1] // 2
    split = (3, n, 2, PLANES, 1024)
    flat = (3, n, 8, 1024)
    vmem = pl.BlockSpec(memory_space=pltpu.VMEM)
    hbm = pl.BlockSpec(memory_space=pl.ANY)
    return pl.pallas_call(
        relax_kernel,
        out_shape=(
            jax.ShapeDtypeStruct(flat, f32),
            jax.ShapeDtypeStruct(flat, f32),
            jax.ShapeDtypeStruct((4, 8, 128), f32),
        ),
        in_specs=[hbm] * 4,
        out_specs=[vmem, vmem, vmem],
        scratch_shapes=[
            pltpu.VMEM(flat, bf16),
            pltpu.VMEM(flat, bf16),
            pltpu.SemaphoreType.DMA((BLOCKS, 4)),
            pltpu.SemaphoreType.DMA((2,)),
        ],
        compiler_params=pltpu.CompilerParams(vmem_limit_bytes=24 << 20),
        cost_estimate=pl.CostEstimate(flops=10_000_000, bytes_accessed=8_000_000, transcendentals=0),
    )(*(in_hbm(x) for x in (velocity, pressure, fields.reshape(split), brownian.reshape(split))))


def stretch(f, base, g):
    return [base[o] + (g[3 * o] * f[0] + g[3 * o + 1] * f[1] + g[3 * o + 2] * f[2]) for o in range(3)]


def share_kernel(
    slabs, near_ref, local_ref, f_ref, base_ref, nf_hbm, own_ref, outer_ref, inner_ref, n_buf, grad, sums, sem
):
    pairs = f_ref.shape[1]
    slab = lax.axis_index("mesh")
    mine = lax.axis_index("field")
    masks = lane_masks()

    planes = [(1, 1), (0, 0), (1, 0), (2, 0), (3, 0), (3, 1)]
    for q in range(PLANES):
        for a in range(3):
            before, centre, after = (near_ref[d, e, a] for d, e in planes[q : q + 3])
            slopes = ((after - before) * 0.5, slope_y(centre, masks), slope_z(centre, masks))
            for c in range(3):
                value = slopes[c] * TIME_STEP
                grad[3 * a + c, pl.ds(q, 8, stride=8), :] = value
                grad[3 * a + c, pl.ds(q + 4, 8, stride=8), :] = value

    def block(j, carry):
        rows = pl.ds(pl.multiple_of(8 * j, 8), 8)
        lanes = lanes_of(j)
        g = [grad[k, rows, :] for k in range(9)]

        def some(i, acc):
            for u in range(UNROLL):
                n = i * UNROLL + u
                f = [f_ref[c, n, :, lanes] for c in range(3)]
                a = stretch(f, [base_ref[o, n, :, lanes] for o in range(3)], g)
                for c in range(3):
                    n_buf[c, n, :, lanes] = a[c].astype(bf16)
                s = [x * x for x in a]
                r = pltpu.reciprocal(MAX_STRETCH - (s[0] + s[1] + s[2]))
                p0 = r * a[0]
                p1 = r * a[1]
                products = (r * s[0], p0 * a[1], p0 * a[2], r * s[1], p1 * a[2], r * s[2])
                acc = tuple(x + y for x, y in zip(acc, products))
            return acc

        acc = lax.fori_loop(0, pairs // UNROLL, some, tuple(jnp.zeros((8, 128), f32) for _ in range(6)))
        for k in range(6):
            sums[k, rows, :] = acc[k]
        for copy in stores(j, n_buf, nf_hbm, sem):
            copy.start()
        return carry

    lax.fori_loop(0, BLOCKS, block, 0)

    scale = VISCOSITY / WEISSENBERG / NF * MAX_STRETCH
    stress = []
    for k in range(6):
        rows = []
        for q in range(PLANES):
            total = sums[k, pl.ds(q, 8, stride=8), :] + sums[k, pl.ds(q + 4, 8, stride=8), :]
            total = total * scale
            if k in DIAGONAL_PAIRS:
                total = total - VISCOSITY / WEISSENBERG / 4
            rows.append(total)
        stress.append(rows)

    own = [mine == q for q in range(PLANES)]
    zero = jnp.zeros((8, 128), f32)
    pressure = [jnp.where(own[q], local_ref[3], 0.0) for q in range(PLANES)]
    start = [[jnp.where(own[q], local_ref[a], 0.0) for q in range(PLANES)] for a in range(3)]

    def at(values, q):
        return values[q] if 0 <= q < PLANES else None

    def add(x, y):
        return y if x is None else x if y is None else x + y

    def halfway(values, q):
        plus, minus = at(values, q + 1), at(values, q - 1)
        if plus is None:
            return None if minus is None else minus * -0.5
        return plus * 0.5 if minus is None else (plus - minus) * 0.5

    first = -(SWEEPS)
    count = PLANES + 2 * SWEEPS
    fluid = []
    for q in range(first, first + count):
        plane = slab * PLANES + q
        inside = (plane >= 0) & (plane < slabs * PLANES)
        wide = plane < slabs * PLANES // 2
        value = jnp.where(masks["channel"] | wide, 1.0 / DIAGONAL, 0.0)
        fluid.append(jnp.where(inside, value, 0.0))

    sources, currents = [], [{q: start[a][q] for q in range(PLANES)} for a in range(3)]
    for a in range(3):
        source = {}
        for q in range(-1, PLANES + 1):
            total = halfway(stress[INDEX[a][0]], q)
            if a == 0:
                total = total - halfway(pressure, q) if total is not None else None
            if 0 <= q < PLANES:
                inner = slope_y(stress[INDEX[a][1]][q], masks) + slope_z(stress[INDEX[a][2]][q], masks)
                if a == 1:
                    inner = inner - slope_y(pressure[q], masks)
                if a == 2:
                    inner = inner - slope_z(pressure[q], masks)
                total = total + inner + start[a][q] * (1.0 / TIME_STEP)
            source[q] = total
        sources.append(source)
    for sweep in range(SWEEPS):
        for a in range(3):
            current = currents[a]
            later = {}
            for q in range(-1 - sweep, PLANES + 1 + sweep):
                total = sources[a].get(q)
                along = add(current.get(q - 1), current.get(q + 1))
                if along is not None:
                    total = add(total, AXIAL * along)
                if q in current:
                    total = add(total, TRANSVERSE * around(current[q], masks))
                later[q] = total * fluid[q - first]
            currents[a] = later
    odd = slab % 2 == 1
    for a in range(3):
        for q in range(PLANES):
            before, after = currents[a][q - PLANES], currents[a][q + PLANES]
            own_ref[q, a] = currents[a][q]
            outer_ref[q, a] = jnp.where(odd, after, before)
            inner_ref[q, a] = jnp.where(odd, before, after)

    def end(j, carry):
        for copy in stores(j, n_buf, nf_hbm, sem):
            copy.wait()
        return carry

    lax.fori_loop(0, BLOCKS, end, 0)


def share(near, local, f_flat, base):
    n = f_flat.shape[1]
    slabs = lax.axis_size("mesh")
    vmem = pl.BlockSpec(memory_space=pltpu.VMEM)
    part = jax.ShapeDtypeStruct((PLANES, 3, 8, 128), f32)
    return pl.pallas_call(
        functools.partial(share_kernel, slabs),
        out_shape=(jax.ShapeDtypeStruct((3, n, 2, PLANES, 1024), bf16), part, part, part),
        in_specs=[vmem] * 4,
        out_specs=[pl.BlockSpec(memory_space=pl.ANY), vmem, vmem, vmem],
        scratch_shapes=[
            pltpu.VMEM((3, n, 8, 1024), bf16),
            pltpu.VMEM((9, 64, 128), f32),
            pltpu.VMEM((6, 64, 128), f32),
            pltpu.SemaphoreType.DMA((BLOCKS, 2)),
        ],
        compiler_params=pltpu.CompilerParams(vmem_limit_bytes=16 << 20),
        cost_estimate=pl.CostEstimate(flops=13_000_000, bytes_accessed=7_000_000, transcendentals=0),
    )(near, local, f_flat, base)


def body(velocity, pressure, fields, brownian):
    total = lax.axis_size("mesh") * PLANES

    def exchange(x, pairs):
        return lax.ppermute(x, AXES, pairs + [(b, a) for a, b in pairs])

    own = velocity.reshape(3, 8, 128)
    ends = range(PLANES - 1, total - 1, PLANES)
    edge = lax.ppermute(own, AXES, [(i, i + 2) for i in ends] + [(i + 1, i) for i in ends])
    f_flat, base, local = relax(own, pressure.reshape(1, 8, 128), fields, brownian)
    near = lax.all_gather(jnp.stack([own, edge]), "field", axis=0)
    new_fields, kept, outer, inner = share(near, local, f_flat, base)

    outer = exchange(outer, [(i, (i + PLANES) ^ 1) for i in range(total - PLANES) if i // PLANES % 2 == 1])
    couples = [[i, i + PLANES] for i in range(total) if i // PLANES % 2 == 0]
    both = lax.all_gather(inner, AXES, axis=0, axis_index_groups=couples)
    inner = jnp.where(lax.axis_index("mesh") % 2 == 1, both[0], both[1])
    mine = lax.axis_index("field")
    shares = kept + (outer + inner)
    others = lax.dynamic_slice_in_dim(jnp.concatenate([shares, shares]), mine + 1, PLANES - 1, 0)
    parts = lax.all_gather(others, "field", axis=0)
    result = lax.dynamic_index_in_dim(shares, mine, 0, keepdims=False)
    for d in range(1, PLANES):
        result = result + lax.dynamic_index_in_dim(parts[:, PLANES - 1 - d], (mine + d) % PLANES, 0, keepdims=False)
    return new_fields.reshape(fields.shape), result.reshape(velocity.shape)


def solution(mesh):
    placed = (
        P(None, ("mesh", "field"), None),
        P(("mesh", "field"), None),
        P(None, "field", "mesh", None),
        P(None, "field", "mesh", None),
    )
    return jax.shard_map(
        body,
        mesh=mesh,
        in_specs=placed,
        out_specs=(P(None, "field", "mesh", None), P(None, ("mesh", "field"), None)),
        check_vma=False,
    )
```
